128 devices in a mesh: band: 8 (over z, core), lev: 16 (over x, y).
Axes of the slice: x: 4, y: 4, z: 4, core: 2. Of those that a mesh axis runs over, the one named last changes fastest.
Arguments:
- spectral_in: bfloat16 [64, 640, 2, 1281], P('lev', 'band'), may hold values from -4 to 4
- legendre: bfloat16 [640, 128, 1281], P('band', 'lev'), may hold values from -0.15625 to 0.15625
- weights: float32 [128], P('lev'), may hold values from 0.5 to 2
- pair_order: int32 [640], replicated, may hold values from 0 to 639, each once
- row_lat: int32 [128], replicated, may hold values from 0 to 127, each once
- lon_count: int32 [128], replicated, may hold values from 20 to 5136, as said below
Outputs:
- grid_field: float32 [64, 128, 5136], P(None, ('lev', 'band'))
- spectral_out: float32 [64, 640, 2, 1281], P('lev', 'band')
The draws below stay inside these ranges and needn't reach their ends.
Inputs may be any that keep to these rules, and one draw needn't show every extreme that they name: Row i of spectral_in, legendre and spectral_out holds wavenumbers pair_order[i] and 1279 - pair_order[i]; every value appears once. Row r of grid_field and of legendre's second dimension and weights lies on latitude row_lat[r]; every value appears once. `lon_count`: each count is 4 i + 16 for a whole number i of 1 to 1280; some latitude has 5136 longitudes and some has 20.
All inputs are finite; a program needn't handle non-finite values.
Results may differ from the reference program's by a relative error of at most 0.013.
Values may be sent and summed in bfloat16 or wider, within the bound.
No kernel may reach another device: no remote copies, remote signals or barrier semaphores. Data moves between devices by JAX's collectives and lax.ppermute only.
A program may use at most 384 MiB of HBM per device.

```python
import math
import jax
import jax.numpy as jnp
from jax import lax

TRUNC = 1279
COEFS = 1281
PAIRS = 640
LEVELS = 64
NLAT = 128


def draw_lon_count(key, part):
    key = jax.random.fold_in(key, 11)
    first_key, second_key = jax.random.split(key)
    cycles = jax.random.randint(first_key, (NLAT,), 1, TRUNC + 2)
    shuffle = jax.random.permutation(second_key, NLAT)
    cycles = jnp.where(shuffle == 0, TRUNC + 1, jnp.where(shuffle == 1, 1, cycles))
    return (4 * cycles + 16).astype(jnp.int32)


def block_levels(own_key, shape, pieces, low, high):
    level, own = 1.0, jax.random.fold_in(own_key, 6)
    for dim, parts in pieces:
        draws = jnp.exp(jax.random.uniform(jax.random.fold_in(own, dim), (parts,), jnp.float32, low / len(pieces), high / len(pieces)))
        level = level * jnp.repeat(draws, shape[dim] // parts).reshape([-1 if axis == dim else 1 for axis in range(len(shape))])
    return level


def scatter_about(rng, dims, spread, most, cuts=(), kind=jnp.bfloat16):
    values = jax.random.normal(rng, dims, jnp.float32) * spread
    if len(cuts) > 0:
        values = block_levels(rng, dims, cuts, -0.22, 0.18) * values
    return jnp.clip(values, min=-most, max=most).astype(kind)


def setup_inputs(seed: int = 0) -> dict:
    arg_keys = jax.random.split(jax.random.key(seed), 7)
    spectral_in = scatter_about(arg_keys[0], (LEVELS, PAIRS, 2, COEFS), 0.7, 4.0, ((0, 16), (1, 8)))
    legendre = scatter_about(arg_keys[1], (PAIRS, NLAT, COEFS), COEFS ** -0.5, 0.15625, ((0, 8), (1, 16)))
    weights = jnp.clip(jnp.exp(math.log(2.0) - 1.3862944 * jax.random.uniform(arg_keys[2], (NLAT,), jnp.float32) ** block_levels(arg_keys[2], (NLAT,), ((0, 16),), -0.2, 0.2)), 0.5, 2.0)
    pair_order = jax.random.permutation(arg_keys[3], PAIRS).astype(jnp.int32)
    row_lat = jax.random.permutation(arg_keys[4], NLAT).astype(jnp.int32)
    lon_count = draw_lon_count(jax.random.fold_in(arg_keys[6], 71), 0)
    return dict(spectral_in=spectral_in, legendre=legendre, weights=weights, pair_order=pair_order, row_lat=row_lat, lon_count=lon_count)


two_pi = 2.0 * math.pi

def wave_basis(waves, count):
    width = 4 * TRUNC + 20
    blocks = (width + 127) // 128
    coarse = jnp.arange(blocks, dtype=jnp.int32) * 128
    fine = jnp.arange(128, dtype=jnp.int32)
    scale = two_pi / count.astype(jnp.float32)
    alpha = scale * (waves[:, :, None] * coarse[None, None, :] % count).astype(jnp.float32)
    beta = scale * (waves[:, :, None] * fine[None, None, :] % count).astype(jnp.float32)
    cos_a = jnp.cos(alpha)[:, :, :, None]
    sin_a = jnp.sin(alpha)[:, :, :, None]
    cos_b = jnp.cos(beta)[:, :, None, :]
    sin_b = jnp.sin(beta)[:, :, None, :]
    shape = (2, waves.shape[1], blocks * 128)
    cos_full = (cos_a * cos_b - sin_a * sin_b).reshape(shape)[:, :, :width]
    sin_full = (sin_a * cos_b + cos_a * sin_b).reshape(shape)[:, :, :width]
    longitude = jnp.arange(width, dtype=jnp.int32)
    active = (2 * waves[:, :, None] < count) & (longitude[None, None, :] < count)
    kappa = jnp.where(waves == 0, 1.0, 2.0).astype(jnp.float32)
    factor = kappa / jnp.sqrt(count.astype(jnp.float32))
    cosine = jnp.where(active, factor[:, :, None] * cos_full, 0.0)
    sine = jnp.where(active, -factor[:, :, None] * sin_full, 0.0)
    table = jnp.stack([cosine, sine], axis=1)
    table = table.reshape(4 * waves.shape[1], width).astype(jnp.bfloat16)
    return (table, kappa)

def row_step(fourier_row, count, weight, waves):
    table, kappa = wave_basis(waves, count)
    levels = fourier_row.shape[1]
    pairs = fourier_row.shape[2]
    coeffs = jnp.transpose(fourier_row, (1, 0, 2)).reshape(levels, 4 * pairs)
    grid_row = jnp.dot(coeffs, table, preferred_element_type=jnp.float32)
    product = (grid_row * jnp.roll(grid_row, -1, axis=0)).astype(jnp.bfloat16)
    raw = lax.dot_general(product, table, (((1,), (1,)), ((), ())), preferred_element_type=jnp.float32)
    scale = weight / kappa
    scale_full = jnp.broadcast_to(scale[:, None, :], (2, 2, pairs)).reshape(4 * pairs)
    back = (raw * scale_full[None, :]).astype(jnp.bfloat16).reshape(levels, 4, pairs)
    return (grid_row, jnp.transpose(back, (1, 0, 2)))

def reference(spectral_in, legendre, weights, pair_order, row_lat, lon_count):
    levels = spectral_in.shape[0]
    slot_index = jnp.arange(COEFS, dtype=jnp.int32)
    split_at = TRUNC + 1 - pair_order
    first_slot = slot_index[None, :] < split_at[:, None]
    masks = jnp.stack([first_slot, jnp.logical_not(first_slot)], 0)
    waves = jnp.stack([pair_order, TRUNC - pair_order], 0).astype(jnp.int32)

    def inverse_pair(items):
        table_pair, spec_pair, mask_pair = items
        masked = jnp.where(mask_pair[:, None, None, :], spec_pair[None], jnp.zeros((), spec_pair.dtype))
        masked = jnp.transpose(masked, (3, 0, 2, 1)).reshape(COEFS, 4 * levels)
        return jnp.dot(table_pair, masked, preferred_element_type=jnp.float32).astype(jnp.bfloat16)
    fourier = lax.map(inverse_pair, (legendre, jnp.transpose(spectral_in, (1, 0, 2, 3)), jnp.transpose(masks, (1, 0, 2))))
    fourier = jnp.transpose(fourier.reshape(PAIRS, NLAT, 4, levels), (1, 2, 3, 0))
    counts = lon_count[row_lat]

    def one_row(items):
        return row_step(items[0], items[1], items[2], waves)
    grid_rows, returned = lax.map(one_row, (fourier, counts, weights))
    grid_field = jnp.transpose(grid_rows, (1, 0, 2))

    def direct_pair(items):
        table_pair, back_pair, mask_pair = items
        summed = lax.dot_general(table_pair, back_pair.reshape(NLAT, 4 * levels), (((0,), (0,)), ((), ())), preferred_element_type=jnp.float32)
        summed = summed.reshape(COEFS, 2, 2, levels)
        result = jnp.where(mask_pair[0][:, None, None], summed[:, 0], 0.0) + jnp.where(mask_pair[1][:, None, None], summed[:, 1], 0.0)
        return jnp.transpose(result, (2, 1, 0))
    spectral = lax.map(direct_pair, (legendre, jnp.transpose(returned, (3, 0, 1, 2)), jnp.transpose(masks, (1, 0, 2))))
    return (grid_field, jnp.transpose(spectral, (1, 0, 2, 3)))
```

```python
import functools
import math

import jax
import jax.numpy as jnp
from jax import lax
from jax.experimental import pallas as pl
from jax.experimental.pallas import tpu as pltpu
from jax.sharding import PartitionSpec as P

TRUNC = 1279
COEFS = TRUNC + 2
LANES = 128
BLOCKS = (COEFS - 1) // LANES
QUARTER = 11
WIDTH = 4 * TRUNC + 20

f32 = jnp.float32
bf16 = jnp.bfloat16

NT = (((1,), (1,)), ((), ()))


def params(mib=48):
    return pltpu.CompilerParams(vmem_limit_bytes=mib * 1024 * 1024)


def pack_kernel(leg_ref, spec_ref, out_ref):
    pairs = leg_ref.shape[0]
    lane = lax.broadcasted_iota(jnp.int32, (16, LANES), 1)
    tail = jnp.zeros((16, LANES), f32)
    for p in range(pairs):
        table = leg_ref[p].astype(f32)
        spec = jnp.concatenate([spec_ref[l, p].astype(f32) for l in range(4)], axis=0)
        rows = jnp.concatenate([table, spec], axis=0)
        for b in range(BLOCKS):
            out_ref[0, p * BLOCKS + b] = rows[:, b * LANES : (b + 1) * LANES].astype(bf16)
        tail = jnp.where(lane == p, rows[:, COEFS - 1 : COEFS], tail)
    out_ref[0, pairs * BLOCKS] = tail.astype(bf16)


def pack(legendre, spectral):
    pairs_dev = legendre.shape[0]
    pairs = pairs_dev // 16
    return pl.pallas_call(
        pack_kernel,
        grid=(16,),
        in_specs=[
            pl.BlockSpec((pairs, 8, COEFS), lambda d: (d, 0, 0)),
            pl.BlockSpec((4, pairs, 2, COEFS), lambda d: (0, d, 0, 0)),
        ],
        out_specs=pl.BlockSpec((1, pairs * BLOCKS + 1, 16, LANES), lambda d: (d, 0, 0, 0)),
        out_shape=jax.ShapeDtypeStruct((16, pairs * BLOCKS + 1, 16, LANES), bf16),
        compiler_params=params(),
        name="pack",
    )(legendre, spectral)


def gathered(main_ref, tail_ref):
    blocks = [main_ref[:, b].reshape(256, LANES) for b in range(BLOCKS)]
    blocks.append(tail_ref[:, 0].reshape(256, LANES))
    return jnp.concatenate(blocks, axis=1)


def invert_kernel(split_ref, main_ref, tail_ref, pick_ref, out_ref):
    p = pl.program_id(0)
    split = split_ref[p]
    data = gathered(main_ref, tail_ref)
    slot = lax.broadcasted_iota(jnp.int32, (16, data.shape[1]), 1)
    whole = BLOCKS * LANES
    first = (slot < split) & (slot < whole)
    second = ((slot >= split) & (slot < whole)) | (slot == whole + p)
    first = jnp.where(first, 1.0, 0.0).astype(bf16)
    second = jnp.where(second, 1.0, 0.0).astype(bf16)
    shape = (16, 16, data.shape[1])
    apart = data.reshape(shape)
    low = (apart * first[None]).reshape(data.shape)
    high = (apart * second[None]).reshape(data.shape)
    for s, part in enumerate((low, high)):
        full = lax.dot_general(data, part, NT, preferred_element_type=f32)
        rows = full.reshape(16, 16, 256)[:, :8].reshape(128, 256).astype(bf16)
        out_ref[0, s] = jnp.dot(rows, pick_ref[...], preferred_element_type=f32).astype(bf16)


def invert(splits, buffer, pick):
    pairs = splits.shape[0]
    return pl.pallas_call(
        invert_kernel,
        grid=(pairs,),
        in_specs=[
            pl.BlockSpec(memory_space=pltpu.SMEM),
            pl.BlockSpec((16, BLOCKS, 16, LANES), lambda p: (0, p, 0, 0)),
            pl.BlockSpec((16, 1, 16, LANES), lambda p: (0, pairs * BLOCKS, 0, 0)),
            pl.BlockSpec((256, LANES), lambda p: (0, 0)),
        ],
        out_specs=pl.BlockSpec((1, 2, 128, LANES), lambda p: (p, 0, 0, 0)),
        out_shape=jax.ShapeDtypeStruct((pairs, 2, 128, LANES), bf16),
        compiler_params=params(),
        name="invert",
    )(splits, buffer, buffer, pick)


def contract_kernel(split_ref, main_ref, tail_ref, order_ref, spread_ref, back_ref, out_ref):
    p = pl.program_id(0)
    split = split_ref[p]
    data = gathered(main_ref, tail_ref)
    sums = []
    for s in range(2):
        turned = lax.dot_general(order_ref[...], back_ref[0, s], NT, preferred_element_type=f32)
        spread = jnp.dot(turned.astype(bf16), spread_ref[...], preferred_element_type=f32)
        sums.append(jnp.dot(spread.astype(bf16), data, preferred_element_type=f32))
    slot = lax.broadcasted_iota(jnp.int32, sums[0].shape, 1)
    result = jnp.where(slot < split, sums[0], sums[1])
    for b in range(0, BLOCKS, 2):
        left = result[:, b * LANES : (b + 1) * LANES].reshape(16, 8, LANES)
        right = result[:, (b + 1) * LANES : (b + 2) * LANES].reshape(16, 8, LANES)
        both = jnp.concatenate([left, right], axis=1).astype(bf16)
        out_ref[:, pl.ds(p * (BLOCKS // 2) + b // 2, 1)] = both[:, None]
    last = sums[1][:, BLOCKS * LANES :].reshape(16, 8, LANES)
    last = jnp.concatenate([last, last], axis=1)
    lane = lax.broadcasted_iota(jnp.int32, last.shape, 2)
    end = out_ref.shape[1] - 1

    @pl.when(p == 0)
    def _():
        out_ref[:, end] = jnp.where(lane == 0, last, 0.0).astype(bf16)

    @pl.when(p > 0)
    def _():
        out_ref[:, end] = jnp.where(lane == p, last, out_ref[:, end].astype(f32)).astype(bf16)


def contract(splits, buffer, order, spread, back):
    pairs = splits.shape[0]
    out_blocks = pairs * BLOCKS // 2 + 1
    return pl.pallas_call(
        contract_kernel,
        grid=(pairs,),
        in_specs=[
            pl.BlockSpec(memory_space=pltpu.SMEM),
            pl.BlockSpec((16, BLOCKS, 16, LANES), lambda p: (0, p, 0, 0)),
            pl.BlockSpec((16, 1, 16, LANES), lambda p: (0, pairs * BLOCKS, 0, 0)),
            pl.BlockSpec((128, LANES), lambda p: (0, 0)),
            pl.BlockSpec((128, 256), lambda p: (0, 0)),
            pl.BlockSpec((1, 2, 128, LANES), lambda p: (p, 0, 0, 0)),
        ],
        out_specs=pl.BlockSpec((16, out_blocks, 16, LANES), lambda p: (0, 0, 0, 0)),
        out_shape=jax.ShapeDtypeStruct((16, out_blocks, 16, LANES), bf16),
        compiler_params=params(),
        name="contract",
    )(splits, buffer, buffer, order, spread, back)


def unpack_kernel(in_ref, out_ref):
    pairs = out_ref.shape[1]
    last = in_ref[0, in_ref.shape[1] - 1].astype(f32)
    for p in range(pairs):
        for h in range(BLOCKS // 2):
            both = in_ref[0, p * (BLOCKS // 2) + h].astype(f32)
            for side in range(2):
                b = 2 * h + side
                for l in range(4):
                    row = side * 8 + 2 * l
                    out_ref[l, p, :, b * LANES : (b + 1) * LANES] = both[row : row + 2]
        for l in range(4):
            out_ref[l, p, :, COEFS - 1 : COEFS] = last[2 * l : 2 * l + 2, p : p + 1]


def unpack(buffer, pairs):
    blocks = buffer.shape[1]
    return pl.pallas_call(
        unpack_kernel,
        grid=(16,),
        in_specs=[pl.BlockSpec((1, blocks, 16, LANES), lambda d: (d, 0, 0, 0))],
        out_specs=pl.BlockSpec((4, pairs, 2, COEFS), lambda d: (0, d, 0, 0)),
        out_shape=jax.ShapeDtypeStruct((4, 16 * pairs, 2, COEFS), f32),
        compiler_params=params(),
        name="unpack",
    )(buffer)


def turn(whole, part):
    scaled = part * (4.0 / whole)
    nearest = jnp.floor(scaled + 0.5)
    angle = (scaled - nearest) * (math.pi / 2)
    square = angle * angle
    sine = angle + angle * square * (
        -1.6666654611e-1 + square * (8.3321608736e-3 - 1.9515295891e-4 * square)
    )
    cosine = 1.0 - 0.5 * square + square * square * (
        4.166664568298827e-2 + square * (-1.388731625493765e-3 + 2.443315711809948e-5 * square)
    )
    odd = (nearest == 1.0) | (nearest == 3.0)
    cos_base = jnp.where(odd, sine, cosine)
    sin_base = jnp.where(odd, cosine, sine)
    cos_sign = jnp.where((nearest == 1.0) | (nearest == 2.0), -1.0, 1.0)
    sin_sign = jnp.where((nearest == 2.0) | (nearest == 3.0), -1.0, 1.0)
    return cos_base * cos_sign, sin_base * sin_sign


def remainder(value, whole):
    quotient = jnp.floor(value * (1.0 / whole))
    rest = value - quotient * whole
    rest = jnp.where(rest < 0.0, rest + whole, rest)
    return jnp.where(rest >= whole, rest - whole, rest)


def basis_kernel(count_ref, order_ref, out_ref):
    whole = count_ref[0].astype(f32)
    order = order_ref[...]
    even = jnp.where(order % 2 == 0, order, TRUNC - order)
    rows = order.shape[0]
    lane = lax.broadcasted_iota(jnp.int32, (rows, LANES), 1).astype(f32)
    for kind in range(2):
        wave = (even if kind == 0 else TRUNC - even).astype(f32)
        cos_fine, sin_fine = turn(whole, remainder(wave * lane, whole))
        cos_coarse, sin_coarse = turn(whole, remainder(wave * (lane * 128.0), whole))
        for a in range(QUARTER):
            cos_a = cos_coarse[:, a : a + 1]
            sin_a = sin_coarse[:, a : a + 1]
            at = pl.ds(a * LANES, LANES)
            out_ref[2 * kind, :, at] = (cos_a * cos_fine - sin_a * sin_fine).astype(bf16)
            out_ref[2 * kind + 1, :, at] = (sin_a * cos_fine + cos_a * sin_fine).astype(bf16)


def basis(count, order):
    pairs = order.shape[0]
    rows = 128
    return pl.pallas_call(
        basis_kernel,
        grid=(pairs // rows,),
        in_specs=[
            pl.BlockSpec(memory_space=pltpu.SMEM),
            pl.BlockSpec((rows, 1), lambda i: (i, 0)),
        ],
        out_specs=pl.BlockSpec((4, rows, QUARTER * LANES), lambda i: (0, i, 0)),
        out_shape=jax.ShapeDtypeStruct((4, pairs, QUARTER * LANES), bf16),
        compiler_params=params(),
        cost_estimate=pl.CostEstimate(flops=200_000_000, bytes_accessed=30_000_000, transcendentals=0),
        name="basis",
    )(count, order)


def grid_kernel(count_ref, weight_ref, order_ref, table_ref, eye_ref, in_ref, grid_ref, back_ref, place):
    count = count_ref[0]
    quarter = count // 4
    whole = jnp.full((1, LANES), count.astype(f32))
    shrink = lax.rsqrt(whole)
    order = order_ref[...]
    pairs = order.shape[0]
    is_even = order % 2 == 0
    even = jnp.where(is_even, order, TRUNC - order)
    odd = TRUNC - even
    lane = lax.broadcasted_iota(jnp.int32, (pairs, LANES), 1)
    left = lane < 64

    def column(condition, yes, no):
        return jnp.broadcast_to(jnp.where(condition, yes, no).astype(f32), (pairs, LANES))

    swap = column(is_even, 1.0, 0.0) > 0.5
    sign_even = column(even % 4 == 0, 1.0, -1.0)
    sign_odd = column(odd % 4 == 1, 1.0, -1.0)
    keep_even = column(2 * even < count, jnp.where(even == 0, 1.0, 2.0), 0.0)
    keep_odd = column(2 * odd < count, 2.0, 0.0)
    first = in_ref[0].astype(f32)
    second = in_ref[1].astype(f32)
    coef_even = jnp.where(swap, first, second) * keep_even
    coef_odd = jnp.where(swap, second, first) * keep_odd
    turned_even = pltpu.roll(coef_even, 64, 1)
    turned_odd = pltpu.roll(coef_odd, 64, 1)
    even_cos = jnp.where(left, coef_even, turned_even * sign_even)
    even_sin = -jnp.where(left, turned_even, coef_even * sign_even)
    odd_cos = jnp.where(left, coef_odd, -(coef_odd * sign_odd))
    odd_sin = -jnp.where(left, turned_odd, turned_odd * sign_odd)

    def upright(values):
        return lax.dot_general(eye_ref[...], values.astype(bf16), NT, preferred_element_type=f32).astype(bf16)

    sum_even = jnp.dot(upright(even_cos), table_ref[0], preferred_element_type=f32)
    sum_even += jnp.dot(upright(even_sin), table_ref[1], preferred_element_type=f32)
    sum_odd = jnp.dot(upright(odd_cos), table_ref[2], preferred_element_type=f32)
    sum_odd += jnp.dot(upright(odd_sin), table_ref[3], preferred_element_type=f32)

    width = QUARTER * LANES
    along = lax.broadcasted_iota(jnp.int32, (1, width), 1)
    factor = jnp.where(along < quarter, jnp.broadcast_to(shrink[:, :1], (1, width)), 0.0)
    near = (sum_even + sum_odd) * factor
    far = (sum_even - sum_odd) * factor

    place[...] = jnp.zeros_like(place)
    narrow = lax.broadcasted_iota(jnp.int32, (64, LANES), 1)
    for t, field in enumerate((near[:64], near[64:], far[:64], far[64:])):
        start = t * quarter
        shift = start % LANES
        base = start // LANES
        before = jnp.zeros((64, LANES), f32)
        for b in range(QUARTER + 1):
            if b < QUARTER:
                block = field[:, b * LANES : (b + 1) * LANES]
                block = pltpu.roll(block, shift, 1)
            else:
                block = jnp.zeros((64, LANES), f32)
            merged = jnp.where(narrow < shift, before, block)
            at = pl.ds(pl.multiple_of((base + b) * LANES, LANES), LANES)
            place[:, at] += merged
            before = block
    grid_ref[...] = place[:, :WIDTH]

    def product(field):
        return jnp.concatenate(
            [
                half * jnp.concatenate([half[1:], half[:1]], axis=0)
                for half in (field[:64], field[64:])
            ],
            axis=0,
        )

    near = product(near)
    far = product(far)
    both = (near + far).astype(bf16)
    gap = (near - far).astype(bf16)

    def analyse(index, values):
        return lax.dot_general(table_ref[index], values, NT, preferred_element_type=f32)

    x_cos = analyse(0, both)
    x_sin = analyse(1, both)
    y_cos = analyse(2, gap)
    y_sin = analyse(3, gap)
    scale = weight_ref[0] * shrink
    back_even = jnp.where(
        left,
        x_cos + sign_even * pltpu.roll(x_cos, 64, 1),
        -(sign_even * x_sin + pltpu.roll(x_sin, 64, 1)),
    )
    turned = pltpu.roll(y_sin, 64, 1)
    back_odd = jnp.where(left, y_cos - sign_odd * turned, -turned - sign_odd * y_cos)
    back_even = jnp.where(keep_even > 0.0, back_even * scale, 0.0)
    back_odd = jnp.where(keep_odd > 0.0, back_odd * scale, 0.0)
    back_ref[0] = jnp.where(swap, back_even, back_odd).astype(bf16)
    back_ref[1] = jnp.where(swap, back_odd, back_even).astype(bf16)


def grid_step(count, weight, order, table, eye, coeffs):
    pairs = order.shape[0]
    smem = pl.BlockSpec(memory_space=pltpu.SMEM)
    vmem = pl.BlockSpec(memory_space=pltpu.VMEM)
    return pl.pallas_call(
        grid_kernel,
        in_specs=[smem, smem, vmem, vmem, vmem, vmem],
        out_specs=[vmem, vmem],
        out_shape=[
            jax.ShapeDtypeStruct((64, WIDTH), f32),
            jax.ShapeDtypeStruct((2, pairs, LANES), bf16),
        ],
        scratch_shapes=[pltpu.VMEM((64, (4 * QUARTER + 2) * LANES), f32)],
        compiler_params=params(),
        name="grid",
    )(count, weight, order, table, eye, coeffs)


def shards(spectral_in, legendre, weights, pair_order, row_lat, lon_count):
    band_count = lax.axis_size("band")
    lev_count = lax.axis_size("lev")
    band_place = lax.axis_index("band")
    lev_place = lax.axis_index("lev")
    devices = band_count * lev_count
    pairs_dev = legendre.shape[0]
    pairs = pairs_dev // lev_count
    all_pairs = pair_order.shape[0]

    buffer = lax.all_to_all(pack(legendre, spectral_in), "lev", 0, 0, tiled=True)

    my_row = lax.dynamic_slice_in_dim(row_lat, lev_place * band_count + band_place, 1)
    my_count = lax.dynamic_slice_in_dim(lon_count, my_row[0], 1)
    my_weight = lax.dynamic_slice_in_dim(weights, band_place, 1)
    my_orders = lax.dynamic_slice_in_dim(pair_order, band_place * pairs_dev + lev_place * pairs, pairs)
    splits = TRUNC + 1 - my_orders
    arrived = pair_order.reshape(band_count, lev_count, pairs).transpose(2, 1, 0).reshape(all_pairs, 1)
    table = basis(my_count, arrived)

    lane = jnp.arange(LANES, dtype=jnp.int32)
    place = 16 * (lane % 64 // 4) + 8 + 2 * (lane % 4) + lane // 64
    pick = (jnp.arange(256, dtype=jnp.int32)[:, None] == place[None, :]).astype(bf16)
    order = ((lane % 2 * 64 + lane // 2)[:, None] == lane[None, :]).astype(bf16)
    spread = ((lane // 8 * 16 + lane % 8)[:, None] == jnp.arange(256, dtype=jnp.int32)[None, :]).astype(bf16)
    eye = (lane[:, None] == lane[None, :]).astype(bf16)

    fourier = invert(splits, buffer, pick)
    fourier = jnp.transpose(fourier, (2, 1, 0, 3)).reshape(devices, 2, pairs * LANES)
    fourier = lax.all_to_all(fourier, ("lev", "band"), 0, 0, tiled=True)
    fourier = fourier.reshape(devices, 2, pairs, LANES).transpose(1, 2, 0, 3).reshape(2, all_pairs, LANES)

    grid_row, back = grid_step(my_count, my_weight, arrived, table, eye, fourier)

    back = back.reshape(2, pairs, devices, LANES).transpose(2, 0, 1, 3).reshape(devices, 2, pairs * LANES)
    back = lax.all_to_all(back, ("lev", "band"), 0, 0, tiled=True)
    back = back.reshape(devices, 2, pairs, LANES).transpose(2, 1, 0, 3)

    spectral = contract(splits, buffer, order, spread, back)
    spectral = lax.all_to_all(spectral, "lev", 0, 0, tiled=True)
    return (grid_row.reshape(64, 1, WIDTH), unpack(spectral, pairs))


def solution(mesh):
    return jax.shard_map(
        shards,
        mesh=mesh,
        in_specs=(P("lev", "band", None, None), P("band", "lev", None), P("lev"), P(), P(), P()),
        out_specs=(P(None, ("lev", "band"), None), P("lev", "band", None, None)),
        check_vma=False,
    )
```

```python
import functools
import math

import jax
import jax.numpy as jnp
from jax import lax
from jax.experimental import pallas as pl
from jax.experimental.pallas import tpu as pltpu
from jax.sharding import PartitionSpec as P

TRUNC = 1279
COEFS = TRUNC + 2
LANES = 128
BLOCKS = (COEFS - 1) // LANES
QUARTER = 11
WIDTH = 4 * TRUNC + 20

f32 = jnp.float32
bf16 = jnp.bfloat16

NT = (((1,), (1,)), ((), ()))


def params(mib=32):
    return pltpu.CompilerParams(vmem_limit_bytes=mib * 1024 * 1024)


def pack_kernel(leg_ref, spec_ref, out_ref):
    dests = out_ref.shape[0]
    pairs = leg_ref.shape[0] // dests
    lane = lax.broadcasted_iota(jnp.int32, (16, LANES), 1)
    for d in range(dests):
        tail = jnp.zeros((16, LANES), f32)
        for p in range(pairs):
            at = d * pairs + p
            table = leg_ref[at].astype(f32)
            spec = jnp.concatenate([spec_ref[l, at].astype(f32) for l in range(4)], axis=0)
            rows = jnp.concatenate([table, spec], axis=0)
            for b in range(BLOCKS):
                out_ref[d, p * BLOCKS + b] = rows[:, b * LANES : (b + 1) * LANES].astype(bf16)
            tail = jnp.where(lane == p, rows[:, COEFS - 1 : COEFS], tail)
        out_ref[d, pairs * BLOCKS] = tail.astype(bf16)


def pack(legendre, spectral):
    pairs = legendre.shape[0] // 16
    dests = 4
    return pl.pallas_call(
        pack_kernel,
        grid=(16 // dests,),
        in_specs=[
            pl.BlockSpec((dests * pairs, 8, COEFS), lambda d: (d, 0, 0)),
            pl.BlockSpec((4, dests * pairs, 2, COEFS), lambda d: (0, d, 0, 0)),
        ],
        out_specs=pl.BlockSpec((dests, pairs * BLOCKS + 1, 16, LANES), lambda d: (d, 0, 0, 0)),
        out_shape=jax.ShapeDtypeStruct((16, pairs * BLOCKS + 1, 16, LANES), bf16),
        compiler_params=params(60),
        name="pack",
    )(legendre, spectral)


def halves(main_ref, tail_ref, which):
    parts = [main_ref[:, b] for b in range(BLOCKS)] + [tail_ref[:, 0]]
    first = which * 8
    return jnp.concatenate(
        [part.astype(f32)[:, first : first + 8].reshape(128, LANES).astype(bf16) for part in parts], axis=1
    )


def invert_kernel(split_ref, main_ref, tail_ref, pick_ref, out_ref, rows_ref):
    p = pl.program_id(0)
    split = split_ref[p]
    table = halves(main_ref, tail_ref, 0)
    data = halves(main_ref, tail_ref, 1)
    slot = lax.broadcasted_iota(jnp.int32, (16, data.shape[1]), 1)
    whole = BLOCKS * LANES
    first = (slot < split) & (slot < whole)
    second = ((slot >= split) & (slot < whole)) | (slot == whole + p)
    apart = data.reshape(8, 16, data.shape[1])
    for s, part in enumerate((first, second)):
        kept = (apart * jnp.where(part, 1.0, 0.0).astype(bf16)[None]).reshape(data.shape)
        sums = lax.dot_general(table, kept, NT, preferred_element_type=f32).astype(bf16)
        sums = jnp.dot(sums, pick_ref[...], preferred_element_type=f32)
        rows_ref[pl.ds(2 * p + s, 128, stride=2 * pl.num_programs(0)), :] = sums

    @pl.when(p == pl.num_programs(0) - 1)
    def _():
        out_ref[...] = rows_ref[...].astype(bf16)


def invert(splits, buffer, pick):
    pairs = splits.shape[0]
    rows = 2 * pairs * 128
    return pl.pallas_call(
        invert_kernel,
        grid=(pairs,),
        in_specs=[
            pl.BlockSpec(memory_space=pltpu.SMEM),
            pl.BlockSpec((16, BLOCKS, 16, LANES), lambda p: (0, p, 0, 0)),
            pl.BlockSpec((16, 1, 16, LANES), lambda p: (0, pairs * BLOCKS, 0, 0)),
            pl.BlockSpec((128, LANES), lambda p: (0, 0)),
        ],
        out_specs=pl.BlockSpec((rows, LANES), lambda p: (0, 0)),
        out_shape=jax.ShapeDtypeStruct((rows, LANES), bf16),
        scratch_shapes=[pltpu.VMEM((rows, LANES), f32)],
        compiler_params=params(),
        name="invert",
    )(splits, buffer, buffer, pick)


def contract_kernel(split_ref, main_ref, tail_ref, order_ref, back_ref, out_ref, rows_ref):
    p = pl.program_id(0)
    split = split_ref[p]

    @pl.when(p == 0)
    def _():
        rows_ref[...] = back_ref[...].astype(f32)

    data = halves(main_ref, tail_ref, 0)
    sums = []
    for s in range(2):
        back = rows_ref[pl.ds(2 * p + s, 128, stride=2 * pl.num_programs(0)), :].astype(bf16)
        turned = lax.dot_general(order_ref[...], back, NT, preferred_element_type=f32).astype(bf16)
        sums.append(jnp.dot(turned, data, preferred_element_type=f32))
    slot = lax.broadcasted_iota(jnp.int32, sums[0].shape, 1)
    result = jnp.where(slot < split, sums[0], sums[1])
    for b in range(0, BLOCKS, 2):
        left = result[:, b * LANES : (b + 1) * LANES].reshape(16, 8, LANES)
        right = result[:, (b + 1) * LANES : (b + 2) * LANES].reshape(16, 8, LANES)
        both = jnp.concatenate([left, right], axis=1).astype(bf16)
        out_ref[:, pl.ds(p * (BLOCKS // 2) + b // 2, 1)] = both[:, None]
    last = sums[1][:, BLOCKS * LANES :].reshape(16, 8, LANES)
    last = jnp.concatenate([last, last], axis=1)
    lane = lax.broadcasted_iota(jnp.int32, last.shape, 2)
    end = out_ref.shape[1] - 1

    @pl.when(p == 0)
    def _():
        out_ref[:, end] = jnp.where(lane == 0, last, 0.0).astype(bf16)

    @pl.when(p > 0)
    def _():
        out_ref[:, end] = jnp.where(lane == p, last, out_ref[:, end].astype(f32)).astype(bf16)


def contract(splits, buffer, order, back):
    pairs = splits.shape[0]
    out_blocks = pairs * BLOCKS // 2 + 1
    rows = 2 * pairs * 128
    return pl.pallas_call(
        contract_kernel,
        grid=(pairs,),
        in_specs=[
            pl.BlockSpec(memory_space=pltpu.SMEM),
            pl.BlockSpec((16, BLOCKS, 16, LANES), lambda p: (0, p, 0, 0)),
            pl.BlockSpec((16, 1, 16, LANES), lambda p: (0, pairs * BLOCKS, 0, 0)),
            pl.BlockSpec((128, LANES), lambda p: (0, 0)),
            pl.BlockSpec((rows, LANES), lambda p: (0, 0)),
        ],
        out_specs=pl.BlockSpec((16, out_blocks, 16, LANES), lambda p: (0, 0, 0, 0)),
        out_shape=jax.ShapeDtypeStruct((16, out_blocks, 16, LANES), bf16),
        scratch_shapes=[pltpu.VMEM((rows, LANES), f32)],
        compiler_params=params(),
        name="contract",
    )(splits, buffer, buffer, order, back)


def unpack_kernel(in_ref, out_ref, rows_ref):
    senders = in_ref.shape[0]
    pairs = out_ref.shape[1] // senders
    blocks = in_ref.shape[1]
    for d in range(senders):
        rows_ref[...] = in_ref[d].astype(f32)
        for p in range(pairs):
            for b in range(BLOCKS):
                for l in range(4):
                    pair = rows_ref[p * (BLOCKS // 2) + b // 2, pl.ds(b % 2 * 8 + 2 * l, 2), :]
                    out_ref[l, d * pairs + p, :, b * LANES : (b + 1) * LANES] = pair
            for l in range(4):
                last = rows_ref[blocks - 1, pl.ds(2 * l, 2), :]
                out_ref[l, d * pairs + p, :, COEFS - 1 : COEFS] = last[:, p : p + 1]


def unpack(buffer, pairs):
    blocks = buffer.shape[1]
    senders = 4
    return pl.pallas_call(
        unpack_kernel,
        grid=(16 // senders,),
        in_specs=[pl.BlockSpec((senders, blocks, 16, LANES), lambda d: (d, 0, 0, 0))],
        out_specs=pl.BlockSpec((4, senders * pairs, 2, COEFS), lambda d: (0, d, 0, 0)),
        out_shape=jax.ShapeDtypeStruct((4, 16 * pairs, 2, COEFS), f32),
        scratch_shapes=[pltpu.VMEM((blocks, 16, LANES), f32)],
        compiler_params=params(),
        name="unpack",
    )(buffer)


def turn(whole, part):
    scaled = part * (4.0 / whole)
    nearest = jnp.floor(scaled + 0.5)
    angle = (scaled - nearest) * (math.pi / 2)
    square = angle * angle
    sine = angle + angle * square * (
        -1.6666654611e-1 + square * (8.3321608736e-3 - 1.9515295891e-4 * square)
    )
    cosine = 1.0 - 0.5 * square + square * square * (
        4.166664568298827e-2 + square * (-1.388731625493765e-3 + 2.443315711809948e-5 * square)
    )
    odd = (nearest == 1.0) | (nearest == 3.0)
    cos_base = jnp.where(odd, sine, cosine)
    sin_base = jnp.where(odd, cosine, sine)
    cos_sign = jnp.where((nearest == 1.0) | (nearest == 2.0), -1.0, 1.0)
    sin_sign = jnp.where((nearest == 2.0) | (nearest == 3.0), -1.0, 1.0)
    return cos_base * cos_sign, sin_base * sin_sign


def remainder(value, whole):
    quotient = jnp.floor(value * (1.0 / whole))
    rest = value - quotient * whole
    rest = jnp.where(rest < 0.0, rest + whole, rest)
    return jnp.where(rest >= whole, rest - whole, rest)


def upright_column(row):
    return jnp.broadcast_to(row.astype(f32), (LANES, LANES)).T


def basis_kernel(count_ref, order_ref, out_ref):
    whole = count_ref[0].astype(f32)
    order = upright_column(order_ref[pl.ds(pl.program_id(0), 1), :])
    rows = LANES
    even = jnp.where(remainder(order, 2.0) < 0.5, order, TRUNC - order)
    lane = lax.broadcasted_iota(jnp.int32, (rows, LANES), 1).astype(f32)
    for kind in range(2):
        wave = even if kind == 0 else TRUNC - even
        cos_fine, sin_fine = turn(whole, remainder(wave * lane, whole))
        cos_coarse, sin_coarse = turn(whole, remainder(wave * (lane * 128.0), whole))
        for a in range(QUARTER):
            cos_a = cos_coarse[:, a : a + 1]
            sin_a = sin_coarse[:, a : a + 1]
            at = pl.ds(a * LANES, LANES)
            out_ref[2 * kind, :, at] = (cos_a * cos_fine - sin_a * sin_fine).astype(bf16)
            out_ref[2 * kind + 1, :, at] = (sin_a * cos_fine + cos_a * sin_fine).astype(bf16)


def basis(count, order):
    rows = LANES
    pairs = order.size
    return pl.pallas_call(
        basis_kernel,
        grid=(pairs // rows,),
        in_specs=[
            pl.BlockSpec(memory_space=pltpu.SMEM),
            pl.BlockSpec(order.shape, lambda i: (0, 0)),
        ],
        out_specs=pl.BlockSpec((4, rows, QUARTER * LANES), lambda i: (0, i, 0)),
        out_shape=jax.ShapeDtypeStruct((4, pairs, QUARTER * LANES), bf16),
        compiler_params=params(),
        cost_estimate=pl.CostEstimate(flops=200_000_000, bytes_accessed=30_000_000, transcendentals=0),
        name="basis",
    )(count, order)


def grid_kernel(count_ref, weight_ref, order_ref, table_ref, eye_ref, in_ref, grid_ref, back_ref, place, rows_ref):
    count = count_ref[0]
    quarter = count // 4
    length = count.astype(f32)
    whole = jnp.full((1, LANES), length)
    shrink = lax.rsqrt(whole)
    groups = order_ref.shape[0]
    pairs = groups * LANES
    order = jnp.concatenate([upright_column(order_ref[pl.ds(i, 1), :]) for i in range(groups)], axis=0)
    swap = remainder(order, 2.0) < 0.5
    even = jnp.where(swap, order, TRUNC - order)
    odd = TRUNC - even
    left = lax.broadcasted_iota(jnp.int32, (pairs, LANES), 1) < 64
    sign_even = jnp.where(remainder(even, 4.0) < 0.5, 1.0, -1.0)
    sign_odd = jnp.where(remainder(odd, 4.0) < 1.5, 1.0, -1.0)
    keep_even = jnp.where(2.0 * even < length, jnp.where(even < 0.5, 1.0, 2.0), 0.0)
    keep_odd = jnp.where(2.0 * odd < length, 2.0, 0.0)
    rows_ref[...] = in_ref[...].astype(f32)

    def arrived(s):
        parts = [rows_ref[pl.ds(2 * i + s, LANES, stride=2 * groups), :] for i in range(groups)]
        return jnp.concatenate(parts, axis=0)

    first = arrived(0)
    second = arrived(1)
    coef_even = jnp.where(swap, first, second) * keep_even
    coef_odd = jnp.where(swap, second, first) * keep_odd
    turned_even = pltpu.roll(coef_even, 64, 1)
    turned_odd = pltpu.roll(coef_odd, 64, 1)
    even_cos = jnp.where(left, coef_even, turned_even * sign_even)
    even_sin = -jnp.where(left, turned_even, coef_even * sign_even)
    odd_cos = jnp.where(left, coef_odd, -(coef_odd * sign_odd))
    odd_sin = -jnp.where(left, turned_odd, turned_odd * sign_odd)

    def upright(values):
        return lax.dot_general(eye_ref[...], values.astype(bf16), NT, preferred_element_type=f32).astype(bf16)

    sum_even = jnp.dot(upright(even_cos), table_ref[0], preferred_element_type=f32)
    sum_even += jnp.dot(upright(even_sin), table_ref[1], preferred_element_type=f32)
    sum_odd = jnp.dot(upright(odd_cos), table_ref[2], preferred_element_type=f32)
    sum_odd += jnp.dot(upright(odd_sin), table_ref[3], preferred_element_type=f32)

    width = QUARTER * LANES
    along = lax.broadcasted_iota(jnp.int32, (1, width), 1)
    factor = jnp.where(along < quarter, jnp.broadcast_to(shrink[:, :1], (1, width)), 0.0)
    near = (sum_even + sum_odd) * factor
    far = (sum_even - sum_odd) * factor

    place[...] = jnp.zeros_like(place)
    narrow = lax.broadcasted_iota(jnp.int32, (64, LANES), 1)
    for t, field in enumerate((near[:64], near[64:], far[:64], far[64:])):
        start = t * quarter
        shift = start % LANES
        base = start // LANES
        before = jnp.zeros((64, LANES), f32)
        for b in range(QUARTER + 1):
            if b < QUARTER:
                block = field[:, b * LANES : (b + 1) * LANES]
                block = pltpu.roll(block, shift, 1)
            else:
                block = jnp.zeros((64, LANES), f32)
            merged = jnp.where(narrow < shift, before, block)
            at = pl.ds(pl.multiple_of((base + b) * LANES, LANES), LANES)
            place[:, at] += merged
            before = block
    grid_ref[...] = place[:, :WIDTH]

    def product(field):
        return jnp.concatenate(
            [
                half * jnp.concatenate([half[1:], half[:1]], axis=0)
                for half in (field[:64], field[64:])
            ],
            axis=0,
        )

    near = product(near)
    far = product(far)
    both = (near + far).astype(bf16)
    gap = (near - far).astype(bf16)

    def analyse(index, values):
        return lax.dot_general(table_ref[index], values, NT, preferred_element_type=f32)

    x_cos = analyse(0, both)
    x_sin = analyse(1, both)
    y_cos = analyse(2, gap)
    y_sin = analyse(3, gap)
    scale = weight_ref[0] * shrink
    back_even = jnp.where(
        left,
        x_cos + sign_even * pltpu.roll(x_cos, 64, 1),
        -(sign_even * x_sin + pltpu.roll(x_sin, 64, 1)),
    )
    turned = pltpu.roll(y_sin, 64, 1)
    back_odd = jnp.where(left, y_cos - sign_odd * turned, -turned - sign_odd * y_cos)
    back_even = jnp.where(keep_even > 0.0, back_even * scale, 0.0)
    back_odd = jnp.where(keep_odd > 0.0, back_odd * scale, 0.0)
    leaving = (jnp.where(swap, back_even, back_odd), jnp.where(swap, back_odd, back_even))
    for s in range(2):
        for i in range(groups):
            part = leaving[s][i * LANES : (i + 1) * LANES]
            rows_ref[pl.ds(2 * i + s, LANES, stride=2 * groups), :] = part
    back_ref[...] = rows_ref[...].astype(bf16)


def grid_step(count, weight, order, table, eye, coeffs):
    rows = 2 * order.size
    smem = pl.BlockSpec(memory_space=pltpu.SMEM)
    vmem = pl.BlockSpec(memory_space=pltpu.VMEM)
    return pl.pallas_call(
        grid_kernel,
        in_specs=[smem, smem, vmem, vmem, vmem, vmem],
        out_specs=[vmem, vmem],
        out_shape=[
            jax.ShapeDtypeStruct((64, WIDTH), f32),
            jax.ShapeDtypeStruct((rows, LANES), bf16),
        ],
        scratch_shapes=[
            pltpu.VMEM((64, (4 * QUARTER + 2) * LANES), f32),
            pltpu.VMEM((rows, LANES), f32),
        ],
        compiler_params=params(),
        name="grid",
    )(count, weight, order, table, eye, coeffs)


def shards(spectral_in, legendre, weights, pair_order, row_lat, lon_count):
    band_count = lax.axis_size("band")
    lev_count = lax.axis_size("lev")
    band_place = lax.axis_index("band")
    lev_place = lax.axis_index("lev")
    devices = band_count * lev_count
    pairs_dev = legendre.shape[0]
    pairs = pairs_dev // lev_count
    all_pairs = pair_order.shape[0]

    buffer = lax.all_to_all(pack(legendre, spectral_in), "lev", 0, 0, tiled=True)

    my_row = lax.dynamic_slice_in_dim(row_lat, lev_place * band_count + band_place, 1)
    my_count = lax.dynamic_slice_in_dim(lon_count, my_row[0], 1)
    my_weight = lax.dynamic_slice_in_dim(weights, band_place, 1)
    my_orders = lax.dynamic_slice_in_dim(pair_order, band_place * pairs_dev + lev_place * pairs, pairs)
    splits = TRUNC + 1 - my_orders
    arrived = pair_order.reshape(band_count, lev_count, pairs).transpose(2, 1, 0).reshape(pairs, devices)
    table = basis(my_count, arrived)

    lane = jnp.arange(LANES, dtype=jnp.int32)
    pick = (lane[:, None] == (2 * (lane % 64) + lane // 64)[None, :]).astype(bf16)
    eye = (lane[:, None] == lane[None, :]).astype(bf16)

    def exchange(rows):
        rows = rows.reshape(devices, pairs, 2, LANES)
        return lax.all_to_all(rows, ("lev", "band"), 0, 0, tiled=True).reshape(2 * all_pairs, LANES)

    fourier = exchange(invert(splits, buffer, pick))
    grid_row, back = grid_step(my_count, my_weight, arrived, table, eye, fourier)
    spectral = contract(splits, buffer, pick, exchange(back))
    spectral = lax.all_to_all(spectral, "lev", 0, 0, tiled=True)
    return (grid_row.reshape(64, 1, WIDTH), unpack(spectral, pairs))


def solution(mesh):
    return jax.shard_map(
        shards,
        mesh=mesh,
        in_specs=(P("lev", "band", None, None), P("band", "lev", None), P("lev"), P(), P(), P()),
        out_specs=(P(None, ("lev", "band"), None), P("lev", "band", None, None)),
        check_vma=False,
    )
```

```python
import functools
import math

import jax
import jax.numpy as jnp
from jax import lax
from jax.experimental import pallas as pl
from jax.experimental.pallas import tpu as pltpu
from jax.sharding import PartitionSpec as P

TRUNC = 1279
COEFS = TRUNC + 2
LANES = 128
BLOCKS = (COEFS - 1) // LANES
QUARTER = 11
WIDTH = 4 * TRUNC + 20

f32 = jnp.float32
bf16 = jnp.bfloat16

NT = (((1,), (1,)), ((), ()))


def params(mib=32):
    return pltpu.CompilerParams(vmem_limit_bytes=int(mib * 1024 * 1024))


def own_place():
    return lax.axis_index("band"), lax.axis_index("lev")


def own_split(order_ref, pairs):
    band, lev = own_place()
    return TRUNC + 1 - order_ref[(band * lax.axis_size("lev") + lev) * pairs + pl.program_id(0)]


def own_count(row_lat_ref, lon_count_ref):
    band, lev = own_place()
    return lon_count_ref[row_lat_ref[lev * lax.axis_size("band") + band]]


def pick_matrix():
    row = lax.broadcasted_iota(jnp.int32, (LANES, LANES), 0)
    lane = lax.broadcasted_iota(jnp.int32, (LANES, LANES), 1)
    return jnp.where(row == 2 * (lane % 64) + lane // 64, 1.0, 0.0).astype(bf16)


def pack_kernel(leg_hbm, spec_hbm, out_ref, leg_ref, spec_ref, sems):
    dests = out_ref.shape[0]
    pairs = leg_ref.shape[0] // dests
    steps = sems.shape[0]
    size = leg_ref.shape[0] // steps
    copies = []
    for i in range(steps):
        part = pl.ds(i * size, size)
        copies.append(
            (
                pltpu.make_async_copy(leg_hbm.at[part], leg_ref.at[part], sems.at[i, 0]),
                pltpu.make_async_copy(spec_hbm.at[:, part], spec_ref.at[:, part], sems.at[i, 1]),
            )
        )
    for pair in copies:
        for copy in pair:
            copy.start()
    lane = lax.broadcasted_iota(jnp.int32, (16, LANES), 1)
    for d in range(dests):
        if d % (dests // steps) == 0:
            for copy in copies[d // (dests // steps)]:
                copy.wait()
        tail = jnp.zeros((16, LANES), f32)
        for p in range(pairs):
            at = d * pairs + p
            table = leg_ref[at].astype(f32)
            spec = jnp.concatenate([spec_ref[l, at].astype(f32) for l in range(4)], axis=0)
            rows = jnp.concatenate([table, spec], axis=0)
            for b in range(BLOCKS):
                out_ref[d, p * BLOCKS + b] = rows[:, b * LANES : (b + 1) * LANES].astype(bf16)
            tail = jnp.where(lane == p, rows[:, COEFS - 1 : COEFS], tail)
        out_ref[d, pairs * BLOCKS] = tail.astype(bf16)


def pack(legendre, spectral):
    pairs = legendre.shape[0] // 16
    hbm = pl.BlockSpec(memory_space=pltpu.HBM)
    return pl.pallas_call(
        pack_kernel,
        in_specs=[hbm, hbm],
        out_specs=pl.BlockSpec(memory_space=pltpu.VMEM),
        out_shape=jax.ShapeDtypeStruct((16, pairs * BLOCKS + 1, 16, LANES), bf16),
        scratch_shapes=[
            pltpu.VMEM(legendre.shape, bf16),
            pltpu.VMEM(spectral.shape, bf16),
            pltpu.SemaphoreType.DMA((8, 2)),
        ],
        compiler_params=params(60),
        name="pack",
    )(legendre, spectral)


def halves(main_ref, tail_ref, which):
    parts = [main_ref[:, b] for b in range(BLOCKS)] + [tail_ref[:, 0]]
    first = which * 8
    return jnp.concatenate(
        [part.astype(f32)[:, first : first + 8].reshape(128, LANES).astype(bf16) for part in parts], axis=1
    )


def invert_kernel(order_ref, main_ref, tail_ref, out_ref, rows_ref):
    p = pl.program_id(0)
    split = own_split(order_ref, pl.num_programs(0))
    pick = pick_matrix()
    table = halves(main_ref, tail_ref, 0)
    data = halves(main_ref, tail_ref, 1)
    slot = lax.broadcasted_iota(jnp.int32, (16, data.shape[1]), 1)
    whole = BLOCKS * LANES
    first = (slot < split) & (slot < whole)
    second = ((slot >= split) & (slot < whole)) | (slot == whole + p)
    apart = data.reshape(8, 16, data.shape[1])
    for s, part in enumerate((first, second)):
        kept = (apart * jnp.where(part, 1.0, 0.0).astype(bf16)[None]).reshape(data.shape)
        sums = lax.dot_general(table, kept, NT, preferred_element_type=f32).astype(bf16)
        sums = jnp.dot(sums, pick, preferred_element_type=f32)
        rows_ref[pl.ds(2 * p + s, 128, stride=2 * pl.num_programs(0)), :] = sums

    @pl.when(p == pl.num_programs(0) - 1)
    def _():
        out_ref[...] = rows_ref[...].astype(bf16)


def invert(order, buffer):
    pairs = buffer.shape[1] // BLOCKS
    rows = 2 * pairs * 128
    return pl.pallas_call(
        invert_kernel,
        grid=(pairs,),
        in_specs=[
            pl.BlockSpec(memory_space=pltpu.SMEM),
            pl.BlockSpec((16, BLOCKS, 16, LANES), lambda p: (0, p, 0, 0)),
            pl.BlockSpec((16, 1, 16, LANES), lambda p: (0, pairs * BLOCKS, 0, 0)),
        ],
        out_specs=pl.BlockSpec((rows, LANES), lambda p: (0, 0)),
        out_shape=jax.ShapeDtypeStruct((rows, LANES), bf16),
        scratch_shapes=[pltpu.VMEM((rows, LANES), f32)],
        compiler_params=params(60.54),
        name="invert",
    )(order, buffer, buffer)


def contract_kernel(order_ref, main_ref, tail_ref, back_ref, out_ref, rows_ref):
    p = pl.program_id(0)
    split = own_split(order_ref, pl.num_programs(0))
    pick = pick_matrix()

    @pl.when(p == 0)
    def _():
        rows_ref[...] = back_ref[...].astype(f32)

    data = halves(main_ref, tail_ref, 0)
    sums = []
    for s in range(2):
        back = rows_ref[pl.ds(2 * p + s, 128, stride=2 * pl.num_programs(0)), :].astype(bf16)
        turned = lax.dot_general(pick, back, NT, preferred_element_type=f32).astype(bf16)
        sums.append(jnp.dot(turned, data, preferred_element_type=f32))
    slot = lax.broadcasted_iota(jnp.int32, sums[0].shape, 1)
    result = jnp.where(slot < split, sums[0], sums[1])
    for b in range(0, BLOCKS, 2):
        left = result[:, b * LANES : (b + 1) * LANES].reshape(16, 8, LANES)
        right = result[:, (b + 1) * LANES : (b + 2) * LANES].reshape(16, 8, LANES)
        both = jnp.concatenate([left, right], axis=1).astype(bf16)
        out_ref[:, pl.ds(p * (BLOCKS // 2) + b // 2, 1)] = both[:, None]
    last = sums[1][:, BLOCKS * LANES :].reshape(16, 8, LANES)
    last = jnp.concatenate([last, last], axis=1)
    lane = lax.broadcasted_iota(jnp.int32, last.shape, 2)
    end = out_ref.shape[1] - 1

    @pl.when(p == 0)
    def _():
        out_ref[:, end] = jnp.where(lane == 0, last, 0.0).astype(bf16)

    @pl.when(p > 0)
    def _():
        out_ref[:, end] = jnp.where(lane == p, last, out_ref[:, end].astype(f32)).astype(bf16)


def contract(order, buffer, back):
    pairs = buffer.shape[1] // BLOCKS
    out_blocks = pairs * BLOCKS // 2 + 1
    rows = 2 * pairs * 128
    return pl.pallas_call(
        contract_kernel,
        grid=(pairs,),
        in_specs=[
            pl.BlockSpec(memory_space=pltpu.SMEM),
            pl.BlockSpec((16, BLOCKS, 16, LANES), lambda p: (0, p, 0, 0)),
            pl.BlockSpec((16, 1, 16, LANES), lambda p: (0, pairs * BLOCKS, 0, 0)),
            pl.BlockSpec((rows, LANES), lambda p: (0, 0)),
        ],
        out_specs=pl.BlockSpec((16, out_blocks, 16, LANES), lambda p: (0, 0, 0, 0)),
        out_shape=jax.ShapeDtypeStruct((16, out_blocks, 16, LANES), bf16),
        scratch_shapes=[pltpu.VMEM((rows, LANES), f32)],
        compiler_params=params(),
        name="contract",
    )(order, buffer, buffer, back)


def unpack_kernel(in_ref, out_ref, rows_ref):
    senders = in_ref.shape[0]
    pairs = out_ref.shape[1] // senders
    blocks = in_ref.shape[1]
    for d in range(senders):
        rows_ref[...] = in_ref[d].astype(f32)
        for p in range(pairs):
            for b in range(BLOCKS):
                for l in range(4):
                    pair = rows_ref[p * (BLOCKS // 2) + b // 2, pl.ds(b % 2 * 8 + 2 * l, 2), :]
                    out_ref[l, d * pairs + p, :, b * LANES : (b + 1) * LANES] = pair
            for l in range(4):
                last = rows_ref[blocks - 1, pl.ds(2 * l, 2), :]
                out_ref[l, d * pairs + p, :, COEFS - 1 : COEFS] = last[:, p : p + 1]


def unpack(buffer, pairs):
    blocks = buffer.shape[1]
    senders = 4
    return pl.pallas_call(
        unpack_kernel,
        grid=(16 // senders,),
        in_specs=[pl.BlockSpec((senders, blocks, 16, LANES), lambda d: (d, 0, 0, 0))],
        out_specs=pl.BlockSpec((4, senders * pairs, 2, COEFS), lambda d: (0, d, 0, 0)),
        out_shape=jax.ShapeDtypeStruct((4, 16 * pairs, 2, COEFS), f32),
        scratch_shapes=[pltpu.VMEM((blocks, 16, LANES), f32)],
        compiler_params=params(),
        name="unpack",
    )(buffer)


def turn(whole, part):
    scaled = part * (4.0 / whole)
    nearest = jnp.floor(scaled + 0.5)
    angle = (scaled - nearest) * (math.pi / 2)
    square = angle * angle
    sine = angle + angle * square * (
        -1.6666654611e-1 + square * (8.3321608736e-3 - 1.9515295891e-4 * square)
    )
    cosine = 1.0 - 0.5 * square + square * square * (
        4.166664568298827e-2 + square * (-1.388731625493765e-3 + 2.443315711809948e-5 * square)
    )
    odd = (nearest == 1.0) | (nearest == 3.0)
    cos_base = jnp.where(odd, sine, cosine)
    sin_base = jnp.where(odd, cosine, sine)
    cos_sign = jnp.where((nearest == 1.0) | (nearest == 2.0), -1.0, 1.0)
    sin_sign = jnp.where((nearest == 2.0) | (nearest == 3.0), -1.0, 1.0)
    return cos_base * cos_sign, sin_base * sin_sign


def remainder(value, whole):
    quotient = jnp.floor(value * (1.0 / whole))
    rest = value - quotient * whole
    rest = jnp.where(rest < 0.0, rest + whole, rest)
    return jnp.where(rest >= whole, rest - whole, rest)


def upright_column(row):
    return jnp.broadcast_to(row.astype(f32), (LANES, LANES)).T


def basis_kernel(row_lat_ref, lon_count_ref, order_ref, out_ref):
    whole = own_count(row_lat_ref, lon_count_ref).astype(f32)
    order = upright_column(order_ref[pl.ds(pl.program_id(0), 1), :])
    rows = LANES
    even = jnp.where(remainder(order, 2.0) < 0.5, order, TRUNC - order)
    lane = lax.broadcasted_iota(jnp.int32, (rows, LANES), 1).astype(f32)
    for kind in range(2):
        wave = even if kind == 0 else TRUNC - even
        cos_fine, sin_fine = turn(whole, remainder(wave * lane, whole))
        cos_coarse, sin_coarse = turn(whole, remainder(wave * (lane * 128.0), whole))
        for a in range(QUARTER):
            cos_a = cos_coarse[:, a : a + 1]
            sin_a = sin_coarse[:, a : a + 1]
            at = pl.ds(a * LANES, LANES)
            out_ref[2 * kind, :, at] = (cos_a * cos_fine - sin_a * sin_fine).astype(bf16)
            out_ref[2 * kind + 1, :, at] = (sin_a * cos_fine + cos_a * sin_fine).astype(bf16)


def basis(row_lat, lon_count, order):
    rows = LANES
    pairs = order.size
    return pl.pallas_call(
        basis_kernel,
        grid=(pairs // rows,),
        in_specs=[
            pl.BlockSpec(memory_space=pltpu.SMEM),
            pl.BlockSpec(memory_space=pltpu.SMEM),
            pl.BlockSpec(order.shape, lambda i: (0, 0)),
        ],
        out_specs=pl.BlockSpec((4, rows, QUARTER * LANES), lambda i: (0, i, 0)),
        out_shape=jax.ShapeDtypeStruct((4, pairs, QUARTER * LANES), bf16),
        compiler_params=params(60),
        cost_estimate=pl.CostEstimate(flops=200_000_000, bytes_accessed=30_000_000, transcendentals=0),
        name="basis",
    )(row_lat, lon_count, order)


def grid_kernel(row_lat_ref, lon_count_ref, weight_ref, order_ref, table_hbm, in_ref, grid_ref, back_ref, place, rows_ref, table_ref, sems):
    loads = [pltpu.make_async_copy(table_hbm.at[i], table_ref.at[i], sems.at[i]) for i in range(4)]
    for load in loads:
        load.start()
    count = own_count(row_lat_ref, lon_count_ref)
    quarter = count // 4
    length = count.astype(f32)
    whole = jnp.full((1, LANES), length)
    shrink = lax.rsqrt(whole)
    groups = order_ref.shape[0]
    pairs = groups * LANES
    order = jnp.concatenate([upright_column(order_ref[pl.ds(i, 1), :]) for i in range(groups)], axis=0)
    swap = remainder(order, 2.0) < 0.5
    even = jnp.where(swap, order, TRUNC - order)
    odd = TRUNC - even
    left = lax.broadcasted_iota(jnp.int32, (pairs, LANES), 1) < 64
    sign_even = jnp.where(remainder(even, 4.0) < 0.5, 1.0, -1.0)
    sign_odd = jnp.where(remainder(odd, 4.0) < 1.5, 1.0, -1.0)
    keep_even = jnp.where(2.0 * even < length, jnp.where(even < 0.5, 1.0, 2.0), 0.0)
    keep_odd = jnp.where(2.0 * odd < length, 2.0, 0.0)
    rows_ref[...] = in_ref[...].astype(f32)

    def arrived(s):
        parts = [rows_ref[pl.ds(2 * i + s, LANES, stride=2 * groups), :] for i in range(groups)]
        return jnp.concatenate(parts, axis=0)

    first = arrived(0)
    second = arrived(1)
    coef_even = jnp.where(swap, first, second) * keep_even
    coef_odd = jnp.where(swap, second, first) * keep_odd
    turned_even = pltpu.roll(coef_even, 64, 1)
    turned_odd = pltpu.roll(coef_odd, 64, 1)
    even_cos = jnp.where(left, coef_even, turned_even * sign_even)
    even_sin = -jnp.where(left, turned_even, coef_even * sign_even)
    odd_cos = jnp.where(left, coef_odd, -(coef_odd * sign_odd))
    odd_sin = -jnp.where(left, turned_odd, turned_odd * sign_odd)

    eye = lax.broadcasted_iota(jnp.int32, (LANES, LANES), 0) == lax.broadcasted_iota(jnp.int32, (LANES, LANES), 1)
    eye = jnp.where(eye, 1.0, 0.0).astype(bf16)

    def upright(values):
        return lax.dot_general(eye, values.astype(bf16), NT, preferred_element_type=f32).astype(bf16)

    sums = []
    for i, values in enumerate((even_cos, even_sin, odd_cos, odd_sin)):
        values = upright(values)
        loads[i].wait()
        sums.append(jnp.dot(values, table_ref[i], preferred_element_type=f32))
    sum_even = sums[0] + sums[1]
    sum_odd = sums[2] + sums[3]

    width = QUARTER * LANES
    along = lax.broadcasted_iota(jnp.int32, (1, width), 1)
    factor = jnp.where(along < quarter, jnp.broadcast_to(shrink[:, :1], (1, width)), 0.0)
    near = (sum_even + sum_odd) * factor
    far = (sum_even - sum_odd) * factor

    place[...] = jnp.zeros_like(place)
    narrow = lax.broadcasted_iota(jnp.int32, (64, LANES), 1)
    for t, field in enumerate((near[:64], near[64:], far[:64], far[64:])):
        start = t * quarter
        shift = start % LANES
        base = start // LANES
        before = jnp.zeros((64, LANES), f32)
        for b in range(QUARTER + 1):
            if b < QUARTER:
                block = field[:, b * LANES : (b + 1) * LANES]
                block = pltpu.roll(block, shift, 1)
            else:
                block = jnp.zeros((64, LANES), f32)
            merged = jnp.where(narrow < shift, before, block)
            at = pl.ds(pl.multiple_of((base + b) * LANES, LANES), LANES)
            place[:, at] += merged
            before = block
    grid_ref[:, 0, :] = place[:, :WIDTH]

    def product(field):
        return jnp.concatenate(
            [
                half * jnp.concatenate([half[1:], half[:1]], axis=0)
                for half in (field[:64], field[64:])
            ],
            axis=0,
        )

    near = product(near)
    far = product(far)
    both = (near + far).astype(bf16)
    gap = (near - far).astype(bf16)

    def analyse(index, values):
        return lax.dot_general(table_ref[index], values, NT, preferred_element_type=f32)

    x_cos = analyse(0, both)
    x_sin = analyse(1, both)
    y_cos = analyse(2, gap)
    y_sin = analyse(3, gap)
    scale = weight_ref[own_place()[0]] * shrink
    back_even = jnp.where(
        left,
        x_cos + sign_even * pltpu.roll(x_cos, 64, 1),
        -(sign_even * x_sin + pltpu.roll(x_sin, 64, 1)),
    )
    turned = pltpu.roll(y_sin, 64, 1)
    back_odd = jnp.where(left, y_cos - sign_odd * turned, -turned - sign_odd * y_cos)
    back_even = jnp.where(keep_even > 0.0, back_even * scale, 0.0)
    back_odd = jnp.where(keep_odd > 0.0, back_odd * scale, 0.0)
    leaving = (jnp.where(swap, back_even, back_odd), jnp.where(swap, back_odd, back_even))
    for s in range(2):
        for i in range(groups):
            part = leaving[s][i * LANES : (i + 1) * LANES]
            rows_ref[pl.ds(2 * i + s, LANES, stride=2 * groups), :] = part
    back_ref[...] = rows_ref[...].astype(bf16)


def grid_step(row_lat, lon_count, weights, order, table, coeffs):
    rows = 2 * order.size
    smem = pl.BlockSpec(memory_space=pltpu.SMEM)
    vmem = pl.BlockSpec(memory_space=pltpu.VMEM)
    return pl.pallas_call(
        grid_kernel,
        in_specs=[smem, smem, smem, vmem, pl.BlockSpec(memory_space=pltpu.HBM), vmem],
        out_specs=[vmem, vmem],
        out_shape=[
            jax.ShapeDtypeStruct((64, 1, WIDTH), f32),
            jax.ShapeDtypeStruct((rows, LANES), bf16),
        ],
        scratch_shapes=[
            pltpu.VMEM((64, (4 * QUARTER + 2) * LANES), f32),
            pltpu.VMEM((rows, LANES), f32),
            pltpu.VMEM(table.shape, bf16),
            pltpu.SemaphoreType.DMA((4,)),
        ],
        compiler_params=params(60),
        name="grid",
    )(row_lat, lon_count, weights, order, table, coeffs)


def shards(spectral_in, legendre, weights, pair_order, row_lat, lon_count):
    band_count = lax.axis_size("band")
    lev_count = lax.axis_size("lev")
    devices = band_count * lev_count
    pairs = legendre.shape[0] // lev_count
    all_pairs = pair_order.shape[0]

    def exchange_pairs(blocks):
        rows = blocks.reshape(lev_count, -1, LANES)
        return lax.all_to_all(rows, "lev", 0, 0, tiled=True).reshape(blocks.shape)

    def exchange_rows(rows):
        rows = rows.reshape(devices, pairs, 2, LANES).transpose(0, 2, 1, 3).reshape(devices, 2, -1)
        rows = lax.all_to_all(rows, ("lev", "band"), 0, 0, tiled=True).reshape(devices, 2, pairs, LANES)
        return rows.transpose(0, 2, 1, 3).reshape(2 * all_pairs, LANES)

    buffer = exchange_pairs(pack(legendre, spectral_in))
    fourier = invert(pair_order, buffer)
    fourier, arrived, row_lat, lon_count = lax.optimization_barrier((fourier, pair_order, row_lat, lon_count))
    arrived = arrived.reshape(band_count, lev_count, pairs).transpose(2, 1, 0).reshape(pairs, devices)
    table = basis(row_lat, lon_count, arrived)
    fourier = exchange_rows(fourier)
    grid_row, back = grid_step(row_lat, lon_count, weights, arrived, table, fourier)
    spectral = exchange_pairs(contract(pair_order, buffer, exchange_rows(back)))
    return (grid_row, unpack(spectral, pairs))


def solution(mesh):
    return jax.shard_map(
        shards,
        mesh=mesh,
        in_specs=(P("lev", "band", None, None), P("band", "lev", None), P("lev"), P(), P(), P()),
        out_specs=(P(None, ("lev", "band"), None), P("lev", "band", None, None)),
        check_vma=False,
    )
```

```python
import functools
import math

import jax
import jax.numpy as jnp
from jax import lax
from jax.experimental import pallas as pl
from jax.experimental.pallas import tpu as pltpu
from jax.sharding import PartitionSpec as P

TRUNC = 1279
COEFS = TRUNC + 2
LANES = 128
BLOCKS = (COEFS - 1) // LANES
QUARTER = 11
WIDTH = 4 * TRUNC + 20

f32 = jnp.float32
bf16 = jnp.bfloat16

NT = (((1,), (1,)), ((), ()))


def params(mib=32):
    return pltpu.CompilerParams(vmem_limit_bytes=int(mib * 1024 * 1024))


def own_place():
    return lax.axis_index("band"), lax.axis_index("lev")


def own_split(order_ref, pairs, p):
    band, lev = own_place()
    return TRUNC + 1 - order_ref[(band * lax.axis_size("lev") + lev) * pairs + p]


def own_count(row_lat_ref, lon_count_ref):
    band, lev = own_place()
    return lon_count_ref[row_lat_ref[lev * lax.axis_size("band") + band]]


def pick_matrix():
    row = lax.broadcasted_iota(jnp.int32, (LANES, LANES), 0)
    lane = lax.broadcasted_iota(jnp.int32, (LANES, LANES), 1)
    return jnp.where(row == 2 * (lane % 64) + lane // 64, 1.0, 0.0).astype(bf16)


def pack_kernel(leg_hbm, spec_hbm, out_hbm, leg_ref, spec_ref, out_ref, in_sems, out_sems):
    dests = out_ref.shape[0]
    pairs = leg_ref.shape[0] // dests
    steps = in_sems.shape[0]
    size = leg_ref.shape[0] // steps
    loads, stores = [], []
    for i in range(steps):
        part = pl.ds(i * size, size)
        loads.append(
            (
                pltpu.make_async_copy(leg_hbm.at[part], leg_ref.at[part], in_sems.at[i, 0]),
                pltpu.make_async_copy(spec_hbm.at[:, part], spec_ref.at[:, part], in_sems.at[i, 1]),
            )
        )
        part = pl.ds(i * (dests // steps), dests // steps)
        stores.append(pltpu.make_async_copy(out_ref.at[part], out_hbm.at[part], out_sems.at[i]))
    for pair in loads:
        for copy in pair:
            copy.start()
    lane = lax.broadcasted_iota(jnp.int32, (16, LANES), 1)
    for i in range(steps):
        for copy in loads[i]:
            copy.wait()
        for d in range(i * (dests // steps), (i + 1) * (dests // steps)):
            tail = jnp.zeros((16, LANES), f32)
            for p in range(pairs):
                at = d * pairs + p
                table = leg_ref[at].astype(f32)
                spec = jnp.concatenate([spec_ref[l, at].astype(f32) for l in range(4)], axis=0)
                rows = jnp.concatenate([table, spec], axis=0)
                for b in range(BLOCKS):
                    out_ref[d, p * BLOCKS + b] = rows[:, b * LANES : (b + 1) * LANES].astype(bf16)
                tail = jnp.where(lane == p, rows[:, COEFS - 1 : COEFS], tail)
            out_ref[d, pairs * BLOCKS] = tail.astype(bf16)
        stores[i].start()
    for store in stores:
        store.wait()


def pack(legendre, spectral):
    pairs = legendre.shape[0] // 16
    out = jax.ShapeDtypeStruct((16, pairs * BLOCKS + 1, 16, LANES), bf16)
    hbm = pl.BlockSpec(memory_space=pltpu.HBM)
    return pl.pallas_call(
        pack_kernel,
        in_specs=[hbm, hbm],
        out_specs=hbm,
        out_shape=out,
        scratch_shapes=[
            pltpu.VMEM(legendre.shape, bf16),
            pltpu.VMEM(spectral.shape, bf16),
            pltpu.VMEM(out.shape, bf16),
            pltpu.SemaphoreType.DMA((8, 2)),
            pltpu.SemaphoreType.DMA((8,)),
        ],
        compiler_params=params(60),
        name="pack",
    )(legendre, spectral)


def halves(buffer_ref, p, which):
    end = buffer_ref.shape[1] - 1
    parts = [buffer_ref[:, p * BLOCKS + b] for b in range(BLOCKS)] + [buffer_ref[:, end]]
    first = which * 8
    return jnp.concatenate(
        [part.astype(f32)[:, first : first + 8].reshape(128, LANES).astype(bf16) for part in parts], axis=1
    )


def invert_kernel(order_ref, buffer_ref, out_ref, rows_ref):
    pairs = buffer_ref.shape[1] // BLOCKS
    pick = pick_matrix()
    whole = BLOCKS * LANES
    for p in range(pairs):
        split = own_split(order_ref, pairs, p)
        table = halves(buffer_ref, p, 0)
        data = halves(buffer_ref, p, 1)
        slot = lax.broadcasted_iota(jnp.int32, (16, data.shape[1]), 1)
        first = (slot < split) & (slot < whole)
        second = ((slot >= split) & (slot < whole)) | (slot == whole + p)
        apart = data.reshape(8, 16, data.shape[1])
        kept = [(apart * jnp.where(part, 1.0, 0.0).astype(bf16)[None]).reshape(data.shape) for part in (first, second)]
        sums = lax.dot_general(table, jnp.concatenate(kept, axis=0), NT, preferred_element_type=f32).astype(bf16)
        for s in range(2):
            part = jnp.dot(sums[:, s * LANES : (s + 1) * LANES], pick, preferred_element_type=f32)
            rows_ref[pl.ds(2 * p + s, 128, stride=2 * pairs), :] = part
    out_ref[...] = rows_ref[...].astype(bf16)


def invert(order, buffer):
    pairs = buffer.shape[1] // BLOCKS
    rows = 2 * pairs * 128
    vmem = pl.BlockSpec(memory_space=pltpu.VMEM)
    return pl.pallas_call(
        invert_kernel,
        in_specs=[pl.BlockSpec(memory_space=pltpu.SMEM), vmem],
        out_specs=vmem,
        out_shape=jax.ShapeDtypeStruct((rows, LANES), bf16),
        scratch_shapes=[pltpu.VMEM((rows, LANES), f32)],
        compiler_params=params(),
        name="invert",
    )(order, buffer)


def contract_kernel(order_ref, buffer_ref, back_ref, out_ref, rows_ref):
    pairs = buffer_ref.shape[1] // BLOCKS
    pick = pick_matrix()
    rows_ref[...] = back_ref[...].astype(f32)
    lane = lax.broadcasted_iota(jnp.int32, (LANES, LANES), 1)
    end = jnp.zeros((LANES, LANES), f32)
    for p in range(pairs):
        split = own_split(order_ref, pairs, p)
        data = halves(buffer_ref, p, 0)
        turned = []
        for s in range(2):
            back = rows_ref[pl.ds(2 * p + s, 128, stride=2 * pairs), :].astype(bf16)
            turned.append(lax.dot_general(pick, back, NT, preferred_element_type=f32).astype(bf16))
        sums = jnp.dot(jnp.concatenate(turned, axis=0), data, preferred_element_type=f32)
        slot = lax.broadcasted_iota(jnp.int32, (LANES, data.shape[1]), 1)
        result = jnp.where(slot < split, sums[:LANES], sums[LANES:])
        for b in range(0, BLOCKS, 2):
            left = result[:, b * LANES : (b + 1) * LANES].reshape(16, 8, LANES)
            right = result[:, (b + 1) * LANES : (b + 2) * LANES].reshape(16, 8, LANES)
            out_ref[:, p * (BLOCKS // 2) + b // 2] = jnp.concatenate([left, right], axis=1).astype(bf16)
        end = jnp.where(lane == p, sums[LANES:, BLOCKS * LANES :], end)
    end = end.reshape(16, 8, LANES)
    out_ref[:, pairs * (BLOCKS // 2)] = jnp.concatenate([end, end], axis=1).astype(bf16)


def contract(order, buffer, back):
    pairs = buffer.shape[1] // BLOCKS
    out_blocks = pairs * BLOCKS // 2 + 1
    vmem = pl.BlockSpec(memory_space=pltpu.VMEM)
    return pl.pallas_call(
        contract_kernel,
        in_specs=[pl.BlockSpec(memory_space=pltpu.SMEM), vmem, vmem],
        out_specs=vmem,
        out_shape=jax.ShapeDtypeStruct((16, out_blocks, 16, LANES), bf16),
        scratch_shapes=[pltpu.VMEM((2 * pairs * 128, LANES), f32)],
        compiler_params=params(),
        name="contract",
    )(order, buffer, back)


def unpack_kernel(in_ref, out_hbm, rows_ref, out_ref, sems):
    senders = in_ref.shape[0]
    pairs = out_ref.shape[1] // senders
    blocks = in_ref.shape[1]
    steps = sems.shape[0]
    stores = []
    for i in range(steps):
        part = pl.ds(i * (senders // steps) * pairs, (senders // steps) * pairs)
        stores.append(pltpu.make_async_copy(out_ref.at[:, part], out_hbm.at[:, part], sems.at[i]))
    for d in range(senders):
        rows = rows_ref.at[d % 2]
        rows[...] = in_ref[d].astype(f32)
        for p in range(pairs):
            for b in range(BLOCKS):
                for l in range(4):
                    pair = rows[p * (BLOCKS // 2) + b // 2, pl.ds(b % 2 * 8 + 2 * l, 2), :]
                    out_ref[l, d * pairs + p, :, b * LANES : (b + 1) * LANES] = pair
            for l in range(4):
                last = rows[blocks - 1, pl.ds(2 * l, 2), :]
                out_ref[l, d * pairs + p, :, COEFS - 1 : COEFS] = last[:, p : p + 1]
        if (d + 1) % (senders // steps) == 0:
            stores[d // (senders // steps)].start()
    for store in stores:
        store.wait()


def unpack(buffer, pairs):
    blocks = buffer.shape[1]
    out = jax.ShapeDtypeStruct((4, 16 * pairs, 2, COEFS), f32)
    return pl.pallas_call(
        unpack_kernel,
        in_specs=[pl.BlockSpec(memory_space=pltpu.VMEM)],
        out_specs=pl.BlockSpec(memory_space=pltpu.HBM),
        out_shape=out,
        scratch_shapes=[
            pltpu.VMEM((2, blocks, 16, LANES), f32),
            pltpu.VMEM(out.shape, f32),
            pltpu.SemaphoreType.DMA((8,)),
        ],
        compiler_params=params(),
        name="unpack",
    )(buffer)


def turn(whole, part):
    scaled = part * (4.0 / whole)
    nearest = jnp.floor(scaled + 0.5)
    angle = (scaled - nearest) * (math.pi / 2)
    square = angle * angle
    sine = angle + angle * square * (
        -1.6666654611e-1 + square * (8.3321608736e-3 - 1.9515295891e-4 * square)
    )
    cosine = 1.0 - 0.5 * square + square * square * (
        4.166664568298827e-2 + square * (-1.388731625493765e-3 + 2.443315711809948e-5 * square)
    )
    odd = (nearest == 1.0) | (nearest == 3.0)
    cos_base = jnp.where(odd, sine, cosine)
    sin_base = jnp.where(odd, cosine, sine)
    cos_sign = jnp.where((nearest == 1.0) | (nearest == 2.0), -1.0, 1.0)
    sin_sign = jnp.where((nearest == 2.0) | (nearest == 3.0), -1.0, 1.0)
    return cos_base * cos_sign, sin_base * sin_sign


def remainder(value, whole):
    quotient = jnp.floor(value * (1.0 / whole))
    rest = value - quotient * whole
    rest = jnp.where(rest < 0.0, rest + whole, rest)
    return jnp.where(rest >= whole, rest - whole, rest)


def upright_column(row):
    return jnp.broadcast_to(row.astype(f32), (LANES, LANES)).T


def basis_kernel(row_lat_ref, lon_count_ref, order_ref, out_ref):
    whole = own_count(row_lat_ref, lon_count_ref).astype(f32)
    order = upright_column(order_ref[pl.ds(pl.program_id(0), 1), :])
    wave = jnp.where(remainder(order, 2.0) < 0.5, order, TRUNC - order)
    lane = lax.broadcasted_iota(jnp.int32, (LANES, LANES), 1).astype(f32)
    cos_fine, sin_fine = turn(whole, remainder(wave * lane, whole))
    cos_coarse, sin_coarse = turn(whole, remainder(wave * (lane * 128.0), whole))
    for a in range(QUARTER):
        cos_a = cos_coarse[:, a : a + 1]
        sin_a = sin_coarse[:, a : a + 1]
        at = pl.ds(a * LANES, LANES)
        out_ref[0, :, at] = (cos_a * cos_fine - sin_a * sin_fine).astype(bf16)
        out_ref[1, :, at] = (sin_a * cos_fine + cos_a * sin_fine).astype(bf16)


def basis(row_lat, lon_count, order):
    rows = LANES
    pairs = order.size
    return pl.pallas_call(
        basis_kernel,
        grid=(pairs // rows,),
        in_specs=[
            pl.BlockSpec(memory_space=pltpu.SMEM),
            pl.BlockSpec(memory_space=pltpu.SMEM),
            pl.BlockSpec(order.shape, lambda i: (0, 0)),
        ],
        out_specs=pl.BlockSpec((2, rows, QUARTER * LANES), lambda i: (0, i, 0)),
        out_shape=jax.ShapeDtypeStruct((2, pairs, QUARTER * LANES), bf16),
        compiler_params=params(60),
        cost_estimate=pl.CostEstimate(flops=200_000_000, bytes_accessed=30_000_000, transcendentals=0),
        name="basis",
    )(row_lat, lon_count, order)


def grid_kernel(row_lat_ref, lon_count_ref, weight_ref, order_ref, table_hbm, in_ref, grid_hbm, back_ref, place, rows_ref, table_ref, grid_ref, sems):
    loads = [pltpu.make_async_copy(table_hbm.at[i], table_ref.at[i], sems.at[i]) for i in range(2)]
    leave = pltpu.make_async_copy(grid_ref, grid_hbm, sems.at[2])
    for load in loads:
        load.start()
    count = own_count(row_lat_ref, lon_count_ref)
    quarter = count // 4
    length = count.astype(f32)
    whole = jnp.full((1, LANES), length)
    shrink = lax.rsqrt(whole)
    groups = order_ref.shape[0]
    pairs = groups * LANES
    order = jnp.concatenate([upright_column(order_ref[pl.ds(i, 1), :]) for i in range(groups)], axis=0)
    swap = remainder(order, 2.0) < 0.5
    even = jnp.where(swap, order, TRUNC - order)
    odd = TRUNC - even
    left = lax.broadcasted_iota(jnp.int32, (pairs, LANES), 1) < 64
    sign_even = jnp.where(remainder(even, 4.0) < 0.5, 1.0, -1.0)
    keep_even = jnp.where(2.0 * even < length, jnp.where(even < 0.5, 1.0, 2.0), 0.0)
    keep_odd = jnp.where(2.0 * odd < length, 2.0, 0.0)
    rows_ref[...] = in_ref[...].astype(f32)

    def arrived(s):
        parts = [rows_ref[pl.ds(2 * i + s, LANES, stride=2 * groups), :] for i in range(groups)]
        return jnp.concatenate(parts, axis=0)

    first = arrived(0)
    second = arrived(1)
    coef_even = jnp.where(swap, first, second) * keep_even
    coef_odd = jnp.where(swap, second, first) * keep_odd
    turned_even = pltpu.roll(coef_even, 64, 1)
    turned_odd = pltpu.roll(coef_odd, 64, 1)
    even_cos = jnp.where(left, coef_even, turned_even * sign_even)
    even_sin = -jnp.where(left, turned_even, coef_even * sign_even)
    odd_cos = jnp.where(left, coef_odd, -coef_odd)
    odd_sin = turned_odd

    eye = lax.broadcasted_iota(jnp.int32, (LANES, LANES), 0) == lax.broadcasted_iota(jnp.int32, (LANES, LANES), 1)
    eye = jnp.where(eye, 1.0, 0.0).astype(bf16)

    def upright(values):
        return lax.dot_general(eye, values.astype(bf16), NT, preferred_element_type=f32).astype(bf16)

    waves = (
        (even_cos, odd_cos, odd_cos * sign_even),
        (even_sin, odd_sin, odd_sin * sign_even),
    )
    sums = 0.0
    for i in range(2):
        values = jnp.concatenate([upright(wave) for wave in waves[i]], axis=0)
        loads[i].wait()
        sums += jnp.dot(values, table_ref[i], preferred_element_type=f32)

    width = QUARTER * LANES
    along = lax.broadcasted_iota(jnp.int32, (1, width), 1)
    factor = jnp.where(along < quarter, jnp.broadcast_to(shrink[:, :1], (1, width)), 0.0)
    place_along = along.astype(f32)
    cos_phase, sin_phase = turn(length, remainder(place_along * float(TRUNC), length))
    sum_even = sums[:128]
    sum_odd = jnp.concatenate(
        [
            cos_phase * sums[128:192] + sin_phase * sums[192:256],
            sin_phase * sums[256:320] - cos_phase * sums[320:],
        ],
        axis=0,
    )
    near = (sum_even + sum_odd) * factor
    far = (sum_even - sum_odd) * factor

    place[...] = jnp.zeros_like(place)
    narrow = lax.broadcasted_iota(jnp.int32, (64, LANES), 1)
    for t, field in enumerate((near[:64], near[64:], far[:64], far[64:])):
        start = t * quarter
        shift = start % LANES
        base = start // LANES
        before = jnp.zeros((64, LANES), f32)
        for b in range(QUARTER + 1):
            if b < QUARTER:
                block = field[:, b * LANES : (b + 1) * LANES]
                block = pltpu.roll(block, shift, 1)
            else:
                block = jnp.zeros((64, LANES), f32)
            merged = jnp.where(narrow < shift, before, block)
            at = pl.ds(pl.multiple_of((base + b) * LANES, LANES), LANES)
            place[:, at] += merged
            before = block
    grid_ref[:, 0, :] = place[:, :WIDTH]
    leave.start()

    def product(field):
        return jnp.concatenate(
            [
                half * jnp.concatenate([half[1:], half[:1]], axis=0)
                for half in (field[:64], field[64:])
            ],
            axis=0,
        )

    near = product(near)
    far = product(far)
    both = near + far
    gap = near - far
    first_cos, first_sin = cos_phase * gap[:64], sin_phase * gap[:64]
    second_cos, second_sin = cos_phase * gap[64:], sin_phase * gap[64:]

    def analyse(index, *parts):
        parts = jnp.concatenate(parts, axis=0).astype(bf16)
        return lax.dot_general(table_ref[index], parts, NT, preferred_element_type=f32)

    by_cos = analyse(0, both, first_cos, -first_sin, second_sin, second_cos)
    by_sin = analyse(1, both, first_sin, first_cos, -second_cos, second_sin)
    x_cos, x_sin = by_cos[:, :LANES], by_sin[:, :LANES]
    y_plain = by_cos[:, LANES : 2 * LANES] + by_sin[:, LANES : 2 * LANES]
    y_signed = by_cos[:, 2 * LANES :] + by_sin[:, 2 * LANES :]
    scale = weight_ref[own_place()[0]] * shrink
    back_even = jnp.where(
        left,
        x_cos + sign_even * pltpu.roll(x_cos, 64, 1),
        -(sign_even * x_sin + pltpu.roll(x_sin, 64, 1)),
    )
    back_odd = y_plain + sign_even * y_signed
    back_even = jnp.where(keep_even > 0.0, back_even * scale, 0.0)
    back_odd = jnp.where(keep_odd > 0.0, back_odd * scale, 0.0)
    leaving = (jnp.where(swap, back_even, back_odd), jnp.where(swap, back_odd, back_even))
    for s in range(2):
        for i in range(groups):
            part = leaving[s][i * LANES : (i + 1) * LANES]
            rows_ref[pl.ds(2 * i + s, LANES, stride=2 * groups), :] = part
    back_ref[...] = rows_ref[...].astype(bf16)
    leave.wait()


def grid_step(row_lat, lon_count, weights, order, table, coeffs):
    rows = 2 * order.size
    smem = pl.BlockSpec(memory_space=pltpu.SMEM)
    vmem = pl.BlockSpec(memory_space=pltpu.VMEM)
    return pl.pallas_call(
        grid_kernel,
        in_specs=[smem, smem, smem, vmem, pl.BlockSpec(memory_space=pltpu.HBM), vmem],
        out_specs=[pl.BlockSpec(memory_space=pltpu.HBM), vmem],
        out_shape=[
            jax.ShapeDtypeStruct((64, 1, WIDTH), f32),
            jax.ShapeDtypeStruct((rows, LANES), bf16),
        ],
        scratch_shapes=[
            pltpu.VMEM((64, (4 * QUARTER + 2) * LANES), f32),
            pltpu.VMEM((rows, LANES), f32),
            pltpu.VMEM(table.shape, bf16),
            pltpu.VMEM((64, 1, WIDTH), f32),
            pltpu.SemaphoreType.DMA((3,)),
        ],
        compiler_params=params(60),
        name="grid",
    )(row_lat, lon_count, weights, order, table, coeffs)


def shards(spectral_in, legendre, weights, pair_order, row_lat, lon_count):
    band_count = lax.axis_size("band")
    lev_count = lax.axis_size("lev")
    devices = band_count * lev_count
    pairs = legendre.shape[0] // lev_count
    all_pairs = pair_order.shape[0]

    def exchange_pairs(blocks):
        rows = blocks.reshape(lev_count, -1, LANES)
        return lax.all_to_all(rows, "lev", 0, 0, tiled=True).reshape(blocks.shape)

    def exchange_rows(rows):
        rows = rows.reshape(devices, pairs, 2, LANES).transpose(0, 2, 1, 3).reshape(devices, 2, -1)
        rows = lax.all_to_all(rows, ("lev", "band"), 0, 0, tiled=True).reshape(devices, 2, pairs, LANES)
        return rows.transpose(0, 2, 1, 3).reshape(2 * all_pairs, LANES)

    buffer = exchange_pairs(pack(legendre, spectral_in))
    fourier = invert(pair_order, buffer)
    fourier, arrived, row_lat, lon_count = lax.optimization_barrier((fourier, pair_order, row_lat, lon_count))
    arrived = arrived.reshape(band_count, lev_count, pairs).transpose(2, 1, 0).reshape(pairs, devices)
    table = basis(row_lat, lon_count, arrived)
    fourier = exchange_rows(fourier)
    grid_row, back = grid_step(row_lat, lon_count, weights, arrived, table, fourier)
    spectral = exchange_pairs(contract(pair_order, buffer, exchange_rows(back)))
    return (grid_row, unpack(spectral, pairs))


def solution(mesh):
    return jax.shard_map(
        shards,
        mesh=mesh,
        in_specs=(P("lev", "band", None, None), P("band", "lev", None), P("lev"), P(), P(), P()),
        out_specs=(P(None, ("lev", "band"), None), P("lev", "band", None, None)),
        check_vma=False,
    )
```

```python
import functools
import math

import jax
import jax.numpy as jnp
from jax import lax
from jax.experimental import pallas as pl
from jax.experimental.pallas import tpu as pltpu
from jax.sharding import PartitionSpec as P

TRUNC = 1279
COEFS = TRUNC + 2
LANES = 128
BLOCKS = (COEFS - 1) // LANES
QUARTER = 11
WIDTH = 4 * TRUNC + 20

f32 = jnp.float32
bf16 = jnp.bfloat16

NT = (((1,), (1,)), ((), ()))


def params(mib=32):
    return pltpu.CompilerParams(vmem_limit_bytes=int(mib * 1024 * 1024))


def own_place():
    return lax.axis_index("band"), lax.axis_index("lev")


def own_split(order_ref, pairs, p):
    band, lev = own_place()
    return TRUNC + 1 - order_ref[(band * lax.axis_size("lev") + lev) * pairs + p]


def own_count(row_lat_ref, lon_count_ref):
    band, lev = own_place()
    return lon_count_ref[row_lat_ref[lev * lax.axis_size("band") + band]]


def pick_matrix():
    row = lax.broadcasted_iota(jnp.int32, (LANES, LANES), 0)
    lane = lax.broadcasted_iota(jnp.int32, (LANES, LANES), 1)
    return jnp.where(row == 2 * (lane % 64) + lane // 64, 1.0, 0.0).astype(bf16)


def pack_kernel(leg_hbm, spec_hbm, out_hbm, leg_ref, spec_ref, out_ref, in_sems, out_sems):
    dests = out_ref.shape[0]
    pairs = leg_ref.shape[0] // dests
    steps = in_sems.shape[0]
    size = leg_ref.shape[0] // steps
    loads, stores = [], []
    for i in range(steps):
        part = pl.ds(i * size, size)
        loads.append(
            (
                pltpu.make_async_copy(leg_hbm.at[part], leg_ref.at[part], in_sems.at[i, 0]),
                pltpu.make_async_copy(spec_hbm.at[:, part], spec_ref.at[:, part], in_sems.at[i, 1]),
            )
        )
        part = pl.ds(dests - (i + 1) * (dests // steps), dests // steps)
        stores.append(pltpu.make_async_copy(out_ref.at[part], out_hbm.at[part], out_sems.at[i]))
    for pair in loads:
        for copy in pair:
            copy.start()
    lane = lax.broadcasted_iota(jnp.int32, (16, LANES), 1)
    for i in range(steps):
        for copy in loads[i]:
            copy.wait()
        for d in range(i * (dests // steps), (i + 1) * (dests // steps)):
            tail = jnp.zeros((16, LANES), f32)
            for p in range(pairs):
                at = d * pairs + p
                table = leg_ref[at].astype(f32)
                spec = jnp.concatenate([spec_ref[l, at].astype(f32) for l in range(4)], axis=0)
                rows = jnp.concatenate([table, spec], axis=0)
                for b in range(BLOCKS):
                    out_ref[dests - 1 - d, p * BLOCKS + b] = rows[:, b * LANES : (b + 1) * LANES].astype(bf16)
                tail = jnp.where(lane == p, rows[:, COEFS - 1 : COEFS], tail)
            out_ref[dests - 1 - d, pairs * BLOCKS] = tail.astype(bf16)
        stores[i].start()
    for store in stores:
        store.wait()


def pack(legendre, spectral):
    pairs = legendre.shape[0] // 16
    out = jax.ShapeDtypeStruct((16, pairs * BLOCKS + 1, 16, LANES), bf16)
    hbm = pl.BlockSpec(memory_space=pltpu.HBM)
    return pl.pallas_call(
        pack_kernel,
        in_specs=[hbm, hbm],
        out_specs=hbm,
        out_shape=out,
        scratch_shapes=[
            pltpu.VMEM(legendre.shape, bf16),
            pltpu.VMEM(spectral.shape, bf16),
            pltpu.VMEM(out.shape, bf16),
            pltpu.SemaphoreType.DMA((8, 2)),
            pltpu.SemaphoreType.DMA((8,)),
        ],
        compiler_params=params(60),
        name="pack",
    )(legendre, spectral)


def halves(buffer_ref, p, which):
    end = buffer_ref.shape[1] - 1
    parts = [buffer_ref[:, p * BLOCKS + b] for b in range(BLOCKS)] + [buffer_ref[:, end]]
    first = which * 8

    def rows(part):
        part = part.astype(f32)[:, first : first + 8]
        return jnp.concatenate([part[d] for d in reversed(range(part.shape[0]))], axis=0).astype(bf16)

    return jnp.concatenate([rows(part) for part in parts], axis=1)


def invert_kernel(order_ref, buffer_ref, out_ref, rows_ref):
    pairs = buffer_ref.shape[1] // BLOCKS
    whole = BLOCKS * LANES
    for p in range(pairs):
        split = own_split(order_ref, pairs, p)
        table = halves(buffer_ref, p, 0)
        data = halves(buffer_ref, p, 1)
        slot = lax.broadcasted_iota(jnp.int32, (16, data.shape[1]), 1)
        first = (slot < split) & (slot < whole)
        second = ((slot >= split) & (slot < whole)) | (slot == whole + p)
        apart = data.reshape(8, 16, data.shape[1])
        kept = [(apart * jnp.where(part, 1.0, 0.0).astype(bf16)[None]).reshape(data.shape) for part in (first, second)]
        sums = lax.dot_general(table, jnp.concatenate(kept, axis=0), NT, preferred_element_type=f32)
        for s in range(2):
            rows_ref[pl.ds(2 * p + s, 128, stride=2 * pairs), :] = sums[:, s * LANES : (s + 1) * LANES]
    rows = rows_ref[...].astype(bf16)
    out_ref[...] = jnp.dot(rows, pick_matrix(), preferred_element_type=f32).astype(bf16)


def invert(order, buffer):
    pairs = buffer.shape[1] // BLOCKS
    rows = 2 * pairs * 128
    vmem = pl.BlockSpec(memory_space=pltpu.VMEM)
    return pl.pallas_call(
        invert_kernel,
        in_specs=[pl.BlockSpec(memory_space=pltpu.SMEM), vmem],
        out_specs=vmem,
        out_shape=jax.ShapeDtypeStruct((rows, LANES), bf16),
        scratch_shapes=[pltpu.VMEM((rows, LANES), f32)],
        compiler_params=params(),
        name="invert",
    )(order, buffer)


def contract_kernel(order_ref, buffer_ref, back_ref, out_ref, rows_ref):
    pairs = buffer_ref.shape[1] // BLOCKS
    rows_ref[...] = back_ref[...].astype(f32)
    apart = [rows_ref[pl.ds(i, 128, stride=2 * pairs), :] for i in range(2 * pairs)]
    apart = jnp.concatenate(apart, axis=0).astype(bf16)
    turned = lax.dot_general(pick_matrix(), apart, NT, preferred_element_type=f32).astype(bf16)
    lane = lax.broadcasted_iota(jnp.int32, (LANES, LANES), 1)
    end = jnp.zeros((LANES, LANES), f32)
    for p in range(pairs):
        split = own_split(order_ref, pairs, p)
        data = halves(buffer_ref, p, 0)
        at = 2 * p * LANES
        back = jnp.concatenate([turned[:, at : at + LANES], turned[:, at + LANES : at + 2 * LANES]], axis=0)
        sums = jnp.dot(back, data, preferred_element_type=f32)
        slot = lax.broadcasted_iota(jnp.int32, (LANES, data.shape[1]), 1)
        result = jnp.where(slot < split, sums[:LANES], sums[LANES:])
        for b in range(0, BLOCKS, 2):
            for d in range(16):
                at = slice(d * 8, (d + 1) * 8)
                left = result[at, b * LANES : (b + 1) * LANES]
                right = result[at, (b + 1) * LANES : (b + 2) * LANES]
                both = jnp.concatenate([left, right], axis=0).astype(bf16)
                out_ref[15 - d, p * (BLOCKS // 2) + b // 2] = both
        end = jnp.where(lane == p, sums[LANES:, BLOCKS * LANES :], end)
    for d in range(16):
        last = end[d * 8 : (d + 1) * 8]
        out_ref[15 - d, pairs * (BLOCKS // 2)] = jnp.concatenate([last, last], axis=0).astype(bf16)


def contract(order, buffer, back):
    pairs = buffer.shape[1] // BLOCKS
    out_blocks = pairs * BLOCKS // 2 + 1
    vmem = pl.BlockSpec(memory_space=pltpu.VMEM)
    return pl.pallas_call(
        contract_kernel,
        in_specs=[pl.BlockSpec(memory_space=pltpu.SMEM), vmem, vmem],
        out_specs=vmem,
        out_shape=jax.ShapeDtypeStruct((16, out_blocks, 16, LANES), bf16),
        scratch_shapes=[pltpu.VMEM((2 * pairs * 128, LANES), f32)],
        compiler_params=params(),
        name="contract",
    )(order, buffer, back)


def unpack_kernel(in_ref, out_hbm, rows_ref, out_ref, sems):
    senders = in_ref.shape[0]
    pairs = out_ref.shape[1] // senders
    blocks = in_ref.shape[1]
    steps = sems.shape[0]
    stores = []
    for i in range(steps):
        part = pl.ds(i * (senders // steps) * pairs, (senders // steps) * pairs)
        stores.append(pltpu.make_async_copy(out_ref.at[:, part], out_hbm.at[:, part], sems.at[i]))
    for d in range(senders):
        rows = rows_ref.at[d % 2]
        rows[...] = in_ref[senders - 1 - d].astype(f32)
        for p in range(pairs):
            for b in range(BLOCKS):
                for l in range(4):
                    pair = rows[p * (BLOCKS // 2) + b // 2, pl.ds(b % 2 * 8 + 2 * l, 2), :]
                    out_ref[l, d * pairs + p, :, b * LANES : (b + 1) * LANES] = pair
            for l in range(4):
                last = rows[blocks - 1, pl.ds(2 * l, 2), :]
                out_ref[l, d * pairs + p, :, COEFS - 1 : COEFS] = last[:, p : p + 1]
        if (d + 1) % (senders // steps) == 0:
            stores[d // (senders // steps)].start()
    for store in stores:
        store.wait()


def unpack(buffer, pairs):
    blocks = buffer.shape[1]
    out = jax.ShapeDtypeStruct((4, 16 * pairs, 2, COEFS), f32)
    return pl.pallas_call(
        unpack_kernel,
        in_specs=[pl.BlockSpec(memory_space=pltpu.VMEM)],
        out_specs=pl.BlockSpec(memory_space=pltpu.HBM),
        out_shape=out,
        scratch_shapes=[
            pltpu.VMEM((2, blocks, 16, LANES), f32),
            pltpu.VMEM(out.shape, f32),
            pltpu.SemaphoreType.DMA((4,)),
        ],
        compiler_params=params(),
        name="unpack",
    )(buffer)


def turn(whole, part):
    scaled = part * (4.0 / whole)
    nearest = jnp.floor(scaled + 0.5)
    angle = (scaled - nearest) * (math.pi / 2)
    square = angle * angle
    sine = angle + angle * square * (
        -1.6666654611e-1 + square * (8.3321608736e-3 - 1.9515295891e-4 * square)
    )
    cosine = 1.0 - 0.5 * square + square * square * (
        4.166664568298827e-2 + square * (-1.388731625493765e-3 + 2.443315711809948e-5 * square)
    )
    odd = (nearest == 1.0) | (nearest == 3.0)
    cos_base = jnp.where(odd, sine, cosine)
    sin_base = jnp.where(odd, cosine, sine)
    cos_sign = jnp.where((nearest == 1.0) | (nearest == 2.0), -1.0, 1.0)
    sin_sign = jnp.where((nearest == 2.0) | (nearest == 3.0), -1.0, 1.0)
    return cos_base * cos_sign, sin_base * sin_sign


def remainder(value, whole):
    quotient = jnp.floor(value * (1.0 / whole))
    rest = value - quotient * whole
    rest = jnp.where(rest < 0.0, rest + whole, rest)
    return jnp.where(rest >= whole, rest - whole, rest)


def upright_column(row):
    return jnp.broadcast_to(row.astype(f32), (LANES, LANES)).T


def basis_kernel(row_lat_ref, lon_count_ref, order_ref, out_ref):
    whole = own_count(row_lat_ref, lon_count_ref).astype(f32)
    order = upright_column(order_ref[pl.ds(pl.program_id(0), 1), :])
    wave = jnp.where(remainder(order, 2.0) < 0.5, order, TRUNC - order)
    lane = lax.broadcasted_iota(jnp.int32, (LANES, LANES), 1).astype(f32)
    cos_fine, sin_fine = turn(whole, remainder(wave * lane, whole))
    cos_coarse, sin_coarse = turn(whole, remainder(wave * (lane * 128.0), whole))
    for a in range(QUARTER):
        cos_a = cos_coarse[:, a : a + 1]
        sin_a = sin_coarse[:, a : a + 1]
        at = pl.ds(a * LANES, LANES)
        out_ref[0, :, at] = (cos_a * cos_fine - sin_a * sin_fine).astype(bf16)
        out_ref[1, :, at] = (sin_a * cos_fine + cos_a * sin_fine).astype(bf16)


def basis(row_lat, lon_count, order):
    rows = LANES
    pairs = order.size
    return pl.pallas_call(
        basis_kernel,
        grid=(pairs // rows,),
        in_specs=[
            pl.BlockSpec(memory_space=pltpu.SMEM),
            pl.BlockSpec(memory_space=pltpu.SMEM),
            pl.BlockSpec(order.shape, lambda i: (0, 0)),
        ],
        out_specs=pl.BlockSpec((2, rows, QUARTER * LANES), lambda i: (0, i, 0)),
        out_shape=jax.ShapeDtypeStruct((2, pairs, QUARTER * LANES), bf16),
        compiler_params=params(60),
        cost_estimate=pl.CostEstimate(flops=200_000_000, bytes_accessed=30_000_000, transcendentals=0),
        name="basis",
    )(row_lat, lon_count, order)


def grid_kernel(row_lat_ref, lon_count_ref, weight_ref, order_ref, table_hbm, in_ref, grid_hbm, back_ref, place, rows_ref, table_ref, grid_ref, sems):
    loads = [pltpu.make_async_copy(table_hbm.at[i], table_ref.at[i], sems.at[i]) for i in range(2)]
    leave = pltpu.make_async_copy(grid_ref, grid_hbm, sems.at[2])
    for load in loads:
        load.start()
    count = own_count(row_lat_ref, lon_count_ref)
    quarter = count // 4
    length = count.astype(f32)
    whole = jnp.full((1, LANES), length)
    shrink = lax.rsqrt(whole)
    groups = order_ref.shape[0]
    pairs = groups * LANES
    order = jnp.concatenate([upright_column(order_ref[pl.ds(i, 1), :]) for i in range(groups)], axis=0)
    swap = remainder(order, 2.0) < 0.5
    even = jnp.where(swap, order, TRUNC - order)
    odd = TRUNC - even
    left = lax.broadcasted_iota(jnp.int32, (pairs, LANES), 1) < 64
    sign_even = jnp.where(remainder(even, 4.0) < 0.5, 1.0, -1.0)
    keep_even = jnp.where(2.0 * even < length, jnp.where(even < 0.5, 1.0, 2.0), 0.0)
    keep_odd = jnp.where(2.0 * odd < length, 2.0, 0.0)
    rows_ref[...] = in_ref[...].astype(f32)

    def arrived(s):
        parts = [rows_ref[pl.ds(2 * i + s, LANES, stride=2 * groups), :] for i in range(groups)]
        return jnp.concatenate(parts, axis=0)

    first = arrived(0)
    second = arrived(1)
    coef_even = jnp.where(swap, first, second) * keep_even
    coef_odd = jnp.where(swap, second, first) * keep_odd
    turned_even = pltpu.roll(coef_even, 64, 1)
    turned_odd = pltpu.roll(coef_odd, 64, 1)
    even_cos = jnp.where(left, coef_even, turned_even * sign_even)
    even_sin = -jnp.where(left, turned_even, coef_even * sign_even)
    odd_cos = jnp.where(left, coef_odd, -coef_odd)
    odd_sin = turned_odd

    eye = lax.broadcasted_iota(jnp.int32, (LANES, LANES), 0) == lax.broadcasted_iota(jnp.int32, (LANES, LANES), 1)
    eye = jnp.where(eye, 1.0, 0.0).astype(bf16)

    def upright(values):
        return lax.dot_general(eye, values.astype(bf16), NT, preferred_element_type=f32).astype(bf16)

    waves = (
        (even_cos, odd_cos, odd_cos * sign_even),
        (even_sin, odd_sin, odd_sin * sign_even),
    )
    sums = 0.0
    for i in range(2):
        values = jnp.concatenate([upright(wave) for wave in waves[i]], axis=0)
        loads[i].wait()
        sums += jnp.dot(values, table_ref[i], preferred_element_type=f32)

    width = QUARTER * LANES
    along = lax.broadcasted_iota(jnp.int32, (1, width), 1)
    factor = jnp.where(along < quarter, jnp.broadcast_to(shrink[:, :1], (1, width)), 0.0)
    place_along = along.astype(f32)
    cos_phase, sin_phase = turn(length, remainder(place_along * float(TRUNC), length))
    sum_even = sums[:128]
    sum_odd = jnp.concatenate(
        [
            cos_phase * sums[128:192] + sin_phase * sums[192:256],
            sin_phase * sums[256:320] - cos_phase * sums[320:],
        ],
        axis=0,
    )
    near = (sum_even + sum_odd) * factor
    far = (sum_even - sum_odd) * factor

    place[...] = jnp.zeros_like(place)
    narrow = lax.broadcasted_iota(jnp.int32, (64, LANES), 1)
    for t, field in enumerate((near[:64], near[64:], far[:64], far[64:])):
        start = t * quarter
        shift = start % LANES
        base = start // LANES
        before = jnp.zeros((64, LANES), f32)
        for b in range(QUARTER + 1):
            if b < QUARTER:
                block = field[:, b * LANES : (b + 1) * LANES]
                block = pltpu.roll(block, shift, 1)
            else:
                block = jnp.zeros((64, LANES), f32)
            merged = jnp.where(narrow < shift, before, block)
            at = pl.ds(pl.multiple_of((base + b) * LANES, LANES), LANES)
            place[:, at] += merged
            before = block
    grid_ref[:, 0, :] = place[:, :WIDTH]
    leave.start()

    def product(field):
        return jnp.concatenate(
            [
                half * jnp.concatenate([half[1:], half[:1]], axis=0)
                for half in (field[:64], field[64:])
            ],
            axis=0,
        )

    near = product(near)
    far = product(far)
    both = near + far
    gap = near - far
    first_cos, first_sin = cos_phase * gap[:64], sin_phase * gap[:64]
    second_cos, second_sin = cos_phase * gap[64:], sin_phase * gap[64:]

    def analyse(index, *parts):
        parts = jnp.concatenate(parts, axis=0).astype(bf16)
        return lax.dot_general(table_ref[index], parts, NT, preferred_element_type=f32)

    by_cos = analyse(0, both, first_cos, -first_sin, second_sin, second_cos)
    by_sin = analyse(1, both, first_sin, first_cos, -second_cos, second_sin)
    x_cos, x_sin = by_cos[:, :LANES], by_sin[:, :LANES]
    y_plain = by_cos[:, LANES : 2 * LANES] + by_sin[:, LANES : 2 * LANES]
    y_signed = by_cos[:, 2 * LANES :] + by_sin[:, 2 * LANES :]
    scale = weight_ref[own_place()[0]] * shrink
    back_even = jnp.where(
        left,
        x_cos + sign_even * pltpu.roll(x_cos, 64, 1),
        -(sign_even * x_sin + pltpu.roll(x_sin, 64, 1)),
    )
    back_odd = y_plain + sign_even * y_signed
    back_even = jnp.where(keep_even > 0.0, back_even * scale, 0.0)
    back_odd = jnp.where(keep_odd > 0.0, back_odd * scale, 0.0)
    leaving = (jnp.where(swap, back_even, back_odd), jnp.where(swap, back_odd, back_even))
    for s in range(2):
        for i in range(groups):
            part = leaving[s][i * LANES : (i + 1) * LANES]
            rows_ref[pl.ds(2 * i + s, LANES, stride=2 * groups), :] = part
    back_ref[...] = rows_ref[...].astype(bf16)
    leave.wait()


def grid_step(row_lat, lon_count, weights, order, table, coeffs):
    rows = 2 * order.size
    smem = pl.BlockSpec(memory_space=pltpu.SMEM)
    vmem = pl.BlockSpec(memory_space=pltpu.VMEM)
    return pl.pallas_call(
        grid_kernel,
        in_specs=[smem, smem, smem, vmem, pl.BlockSpec(memory_space=pltpu.HBM), vmem],
        out_specs=[pl.BlockSpec(memory_space=pltpu.HBM), vmem],
        out_shape=[
            jax.ShapeDtypeStruct((64, 1, WIDTH), f32),
            jax.ShapeDtypeStruct((rows, LANES), bf16),
        ],
        scratch_shapes=[
            pltpu.VMEM((64, (4 * QUARTER + 2) * LANES), f32),
            pltpu.VMEM((rows, LANES), f32),
            pltpu.VMEM(table.shape, bf16),
            pltpu.VMEM((64, 1, WIDTH), f32),
            pltpu.SemaphoreType.DMA((3,)),
        ],
        compiler_params=params(60),
        name="grid",
    )(row_lat, lon_count, weights, order, table, coeffs)


def shards(spectral_in, legendre, weights, pair_order, row_lat, lon_count):
    band_count = lax.axis_size("band")
    lev_count = lax.axis_size("lev")
    devices = band_count * lev_count
    pairs = legendre.shape[0] // lev_count
    all_pairs = pair_order.shape[0]

    def exchange_pairs(blocks):
        rows = blocks.reshape(lev_count, -1, LANES)
        backwards = [list(reversed(range(lev_count)))]
        rows = lax.all_to_all(rows, "lev", 0, 0, tiled=True, axis_index_groups=backwards)
        return rows.reshape(blocks.shape)

    def exchange_rows(rows):
        rows = rows.reshape(devices, pairs, 2, LANES).transpose(0, 2, 1, 3).reshape(devices, 2, -1)
        rows = lax.all_to_all(rows, ("lev", "band"), 0, 0, tiled=True).reshape(devices, 2, pairs, LANES)
        return rows.transpose(0, 2, 1, 3).reshape(2 * all_pairs, LANES)

    buffer = exchange_pairs(pack(legendre, spectral_in))
    fourier = invert(pair_order, buffer)
    fourier, arrived, row_lat, lon_count = lax.optimization_barrier((fourier, pair_order, row_lat, lon_count))
    arrived = arrived.reshape(band_count, lev_count, pairs).transpose(2, 1, 0).reshape(pairs, devices)
    table = basis(row_lat, lon_count, arrived)
    fourier = exchange_rows(fourier)
    grid_row, back = grid_step(row_lat, lon_count, weights, arrived, table, fourier)
    spectral = exchange_pairs(contract(pair_order, buffer, exchange_rows(back)))
    return (grid_row, unpack(spectral, pairs))


def solution(mesh):
    return jax.shard_map(
        shards,
        mesh=mesh,
        in_specs=(P("lev", "band", None, None), P("band", "lev", None), P("lev"), P(), P(), P()),
        out_specs=(P(None, ("lev", "band"), None), P("lev", "band", None, None)),
        check_vma=False,
    )
```

```python
import functools
import math

import jax
import jax.numpy as jnp
from jax import lax
from jax.experimental import pallas as pl
from jax.experimental.pallas import tpu as pltpu
from jax.sharding import PartitionSpec as P

TRUNC = 1279
COEFS = TRUNC + 2
LANES = 128
BLOCKS = (COEFS - 1) // LANES
QUARTER = 11
WIDTH = 4 * TRUNC + 20

f32 = jnp.float32
bf16 = jnp.bfloat16

NT = (((1,), (1,)), ((), ()))


def params(mib=32):
    return pltpu.CompilerParams(vmem_limit_bytes=int(mib * 1024 * 1024))


def own_place():
    return lax.axis_index("band"), lax.axis_index("lev")


def own_split(order_ref, pairs, p):
    band, lev = own_place()
    return TRUNC + 1 - order_ref[(band * lax.axis_size("lev") + lev) * pairs + p]


def own_count(row_lat_ref, lon_count_ref):
    band, lev = own_place()
    return lon_count_ref[row_lat_ref[lev * lax.axis_size("band") + band]]


def pick_matrix():
    row = lax.broadcasted_iota(jnp.int32, (LANES, LANES), 0)
    lane = lax.broadcasted_iota(jnp.int32, (LANES, LANES), 1)
    return jnp.where(row == 2 * (lane % 64) + lane // 64, 1.0, 0.0).astype(bf16)


def pack_kernel(leg_hbm, spec_hbm, out_hbm, leg_ref, spec_ref, out_ref, in_sems, out_sems):
    dests = out_ref.shape[0]
    pairs = leg_ref.shape[0] // dests
    steps = in_sems.shape[0]
    size = leg_ref.shape[0] // steps
    loads, stores = [], []
    for i in range(steps):
        part = pl.ds(i * size, size)
        loads.append(
            (
                pltpu.make_async_copy(leg_hbm.at[part], leg_ref.at[part], in_sems.at[i, 0]),
                pltpu.make_async_copy(spec_hbm.at[:, part], spec_ref.at[:, part], in_sems.at[i, 1]),
            )
        )
        part = pl.ds(dests - (i + 1) * (dests // steps), dests // steps)
        stores.append(pltpu.make_async_copy(out_ref.at[part], out_hbm.at[part], out_sems.at[i]))
    for pair in loads:
        for copy in pair:
            copy.start()
    lane = lax.broadcasted_iota(jnp.int32, (16, LANES), 1)
    for i in range(steps):
        for copy in loads[i]:
            copy.wait()
        for d in range(i * (dests // steps), (i + 1) * (dests // steps)):
            tail = jnp.zeros((16, LANES), f32)
            for p in range(pairs):
                at = d * pairs + p
                table = leg_ref[at].astype(f32)
                spec = jnp.concatenate([spec_ref[l, at].astype(f32) for l in range(4)], axis=0)
                rows = jnp.concatenate([table, spec], axis=0)
                for b in range(BLOCKS):
                    out_ref[dests - 1 - d, p * BLOCKS + b] = rows[:, b * LANES : (b + 1) * LANES].astype(bf16)
                tail = jnp.where(lane == p, rows[:, COEFS - 1 : COEFS], tail)
            out_ref[dests - 1 - d, pairs * BLOCKS] = tail.astype(bf16)
        stores[i].start()
    for store in stores:
        store.wait()


def pack(legendre, spectral):
    pairs = legendre.shape[0] // 16
    out = jax.ShapeDtypeStruct((16, pairs * BLOCKS + 1, 16, LANES), bf16)
    hbm = pl.BlockSpec(memory_space=pltpu.HBM)
    return pl.pallas_call(
        pack_kernel,
        in_specs=[hbm, hbm],
        out_specs=hbm,
        out_shape=out,
        scratch_shapes=[
            pltpu.VMEM(legendre.shape, bf16),
            pltpu.VMEM(spectral.shape, bf16),
            pltpu.VMEM(out.shape, bf16),
            pltpu.SemaphoreType.DMA((8, 2)),
            pltpu.SemaphoreType.DMA((8,)),
        ],
        compiler_params=params(60),
        name="pack",
    )(legendre, spectral)


def halves(buffer_ref, p, which):
    end = buffer_ref.shape[1] - 1
    parts = [buffer_ref[:, p * BLOCKS + b] for b in range(BLOCKS)] + [buffer_ref[:, end]]
    first = which * 8

    def rows(part):
        part = part.astype(f32)[:, first : first + 8]
        return jnp.concatenate([part[d] for d in reversed(range(part.shape[0]))], axis=0).astype(bf16)

    return jnp.concatenate([rows(part) for part in parts], axis=1)


def invert_kernel(order_ref, buffer_ref, out_ref, rows_ref):
    pairs = buffer_ref.shape[1] // BLOCKS
    whole = BLOCKS * LANES
    for p in range(pairs):
        split = own_split(order_ref, pairs, p)
        table = halves(buffer_ref, p, 0)
        data = halves(buffer_ref, p, 1)
        slot = lax.broadcasted_iota(jnp.int32, (16, data.shape[1]), 1)
        first = (slot < split) & (slot < whole)
        second = ((slot >= split) & (slot < whole)) | (slot == whole + p)
        apart = data.reshape(8, 16, data.shape[1])
        kept = [(apart * jnp.where(part, 1.0, 0.0).astype(bf16)[None]).reshape(data.shape) for part in (first, second)]
        sums = lax.dot_general(table, jnp.concatenate(kept, axis=0), NT, preferred_element_type=f32)
        for s in range(2):
            rows_ref[pl.ds(2 * p + s, 128, stride=2 * pairs), :] = sums[:, s * LANES : (s + 1) * LANES]
    rows = rows_ref[...].astype(bf16)
    out_ref[...] = jnp.dot(rows, pick_matrix(), preferred_element_type=f32).astype(bf16)


def invert(order, buffer):
    pairs = buffer.shape[1] // BLOCKS
    rows = 2 * pairs * 128
    vmem = pl.BlockSpec(memory_space=pltpu.VMEM)
    return pl.pallas_call(
        invert_kernel,
        in_specs=[pl.BlockSpec(memory_space=pltpu.SMEM), vmem],
        out_specs=vmem,
        out_shape=jax.ShapeDtypeStruct((rows, LANES), bf16),
        scratch_shapes=[pltpu.VMEM((rows, LANES), f32)],
        compiler_params=params(),
        name="invert",
    )(order, buffer)


def contract_kernel(order_ref, buffer_ref, back_ref, out_ref, rows_ref):
    pairs = buffer_ref.shape[1] // BLOCKS
    rows_ref[...] = back_ref[...].astype(f32)
    apart = [rows_ref[pl.ds(i, 128, stride=2 * pairs), :] for i in range(2 * pairs)]
    apart = jnp.concatenate(apart, axis=0).astype(bf16)
    turned = lax.dot_general(pick_matrix(), apart, NT, preferred_element_type=f32).astype(bf16)
    lane = lax.broadcasted_iota(jnp.int32, (LANES, LANES), 1)
    end = jnp.zeros((LANES, LANES), f32)
    for p in range(pairs):
        split = own_split(order_ref, pairs, p)
        data = halves(buffer_ref, p, 0)
        at = 2 * p * LANES
        back = jnp.concatenate([turned[:, at : at + LANES], turned[:, at + LANES : at + 2 * LANES]], axis=0)
        sums = jnp.dot(back, data, preferred_element_type=f32)
        slot = lax.broadcasted_iota(jnp.int32, (LANES, data.shape[1]), 1)
        result = jnp.where(slot < split, sums[:LANES], sums[LANES:])
        for b in range(0, BLOCKS, 2):
            for d in range(16):
                at = slice(d * 8, (d + 1) * 8)
                left = result[at, b * LANES : (b + 1) * LANES]
                right = result[at, (b + 1) * LANES : (b + 2) * LANES]
                both = jnp.concatenate([left, right], axis=0).astype(bf16)
                out_ref[15 - d, p * (BLOCKS // 2) + b // 2] = both
        end = jnp.where(lane == p, sums[LANES:, BLOCKS * LANES :], end)
    for d in range(16):
        last = end[d * 8 : (d + 1) * 8]
        out_ref[15 - d, pairs * (BLOCKS // 2)] = jnp.concatenate([last, last], axis=0).astype(bf16)


def contract(order, buffer, back):
    pairs = buffer.shape[1] // BLOCKS
    out_blocks = pairs * BLOCKS // 2 + 1
    vmem = pl.BlockSpec(memory_space=pltpu.VMEM)
    return pl.pallas_call(
        contract_kernel,
        in_specs=[pl.BlockSpec(memory_space=pltpu.SMEM), vmem, vmem],
        out_specs=vmem,
        out_shape=jax.ShapeDtypeStruct((16, out_blocks, 16, LANES), bf16),
        scratch_shapes=[pltpu.VMEM((2 * pairs * 128, LANES), f32)],
        compiler_params=params(),
        name="contract",
    )(order, buffer, back)


def unpack_kernel(in_ref, out_hbm, rows_ref, out_ref, sems):
    senders = in_ref.shape[0]
    pairs = out_ref.shape[1] // senders
    blocks = in_ref.shape[1]
    steps = sems.shape[0]
    stores = []
    for i in range(steps):
        part = pl.ds(i * (senders // steps) * pairs, (senders // steps) * pairs)
        stores.append(pltpu.make_async_copy(out_ref.at[:, part], out_hbm.at[:, part], sems.at[i]))
    for d in range(senders):
        rows = rows_ref.at[d % 2]
        rows[...] = in_ref[senders - 1 - d].astype(f32)
        for p in range(pairs):
            for b in range(BLOCKS):
                for l in range(4):
                    pair = rows[p * (BLOCKS // 2) + b // 2, pl.ds(b % 2 * 8 + 2 * l, 2), :]
                    out_ref[l, d * pairs + p, :, b * LANES : (b + 1) * LANES] = pair
            for l in range(4):
                last = rows[blocks - 1, pl.ds(2 * l, 2), :]
                out_ref[l, d * pairs + p, :, COEFS - 1 : COEFS] = last[:, p : p + 1]
        if (d + 1) % (senders // steps) == 0:
            stores[d // (senders // steps)].start()
    for store in stores:
        store.wait()


def unpack(buffer, pairs):
    blocks = buffer.shape[1]
    out = jax.ShapeDtypeStruct((4, 16 * pairs, 2, COEFS), f32)
    return pl.pallas_call(
        unpack_kernel,
        in_specs=[pl.BlockSpec(memory_space=pltpu.VMEM)],
        out_specs=pl.BlockSpec(memory_space=pltpu.HBM),
        out_shape=out,
        scratch_shapes=[
            pltpu.VMEM((2, blocks, 16, LANES), f32),
            pltpu.VMEM(out.shape, f32),
            pltpu.SemaphoreType.DMA((4,)),
        ],
        compiler_params=params(),
        name="unpack",
    )(buffer)


def turn(whole, part):
    scaled = part * (4.0 / whole)
    nearest = jnp.floor(scaled + 0.5)
    angle = (scaled - nearest) * (math.pi / 2)
    square = angle * angle
    sine = angle + angle * square * (
        -1.6666654611e-1 + square * (8.3321608736e-3 - 1.9515295891e-4 * square)
    )
    cosine = 1.0 - 0.5 * square + square * square * (
        4.166664568298827e-2 + square * (-1.388731625493765e-3 + 2.443315711809948e-5 * square)
    )
    odd = (nearest == 1.0) | (nearest == 3.0)
    cos_base = jnp.where(odd, sine, cosine)
    sin_base = jnp.where(odd, cosine, sine)
    cos_sign = jnp.where((nearest == 1.0) | (nearest == 2.0), -1.0, 1.0)
    sin_sign = jnp.where((nearest == 2.0) | (nearest == 3.0), -1.0, 1.0)
    return cos_base * cos_sign, sin_base * sin_sign


def remainder(value, whole):
    quotient = jnp.floor(value * (1.0 / whole))
    rest = value - quotient * whole
    rest = jnp.where(rest < 0.0, rest + whole, rest)
    return jnp.where(rest >= whole, rest - whole, rest)


def upright_column(row):
    return jnp.broadcast_to(row.astype(f32), (LANES, LANES)).T


def basis_kernel(row_lat_ref, lon_count_ref, order_ref, out_ref):
    whole = own_count(row_lat_ref, lon_count_ref).astype(f32)
    order = upright_column(order_ref[pl.ds(pl.program_id(0), 1), :])
    wave = jnp.where(remainder(order, 2.0) < 0.5, order, TRUNC - order)
    lane = lax.broadcasted_iota(jnp.int32, (LANES, LANES), 1).astype(f32)
    cos_fine, sin_fine = turn(whole, remainder(wave * lane, whole))
    cos_coarse, sin_coarse = turn(whole, remainder(wave * (lane * 128.0), whole))
    for a in range(QUARTER):
        cos_a = cos_coarse[:, a : a + 1]
        sin_a = sin_coarse[:, a : a + 1]
        at = pl.ds(a * LANES, LANES)
        out_ref[0, :, at] = (cos_a * cos_fine - sin_a * sin_fine).astype(bf16)
        out_ref[1, :, at] = (sin_a * cos_fine + cos_a * sin_fine).astype(bf16)


def basis(row_lat, lon_count, order):
    rows = LANES
    pairs = order.size
    return pl.pallas_call(
        basis_kernel,
        grid=(pairs // rows,),
        in_specs=[
            pl.BlockSpec(memory_space=pltpu.SMEM),
            pl.BlockSpec(memory_space=pltpu.SMEM),
            pl.BlockSpec(order.shape, lambda i: (0, 0)),
        ],
        out_specs=pl.BlockSpec((2, rows, QUARTER * LANES), lambda i: (0, i, 0)),
        out_shape=jax.ShapeDtypeStruct((2, pairs, QUARTER * LANES), bf16),
        compiler_params=params(60),
        cost_estimate=pl.CostEstimate(flops=200_000_000, bytes_accessed=30_000_000, transcendentals=0),
        name="basis",
    )(row_lat, lon_count, order)


def grid_kernel(row_lat_ref, lon_count_ref, weight_ref, order_ref, table_hbm, in_hbm, grid_hbm, back_ref, place, rows_ref, table_ref, grid_ref, in_ref, sems):
    enter = pltpu.make_async_copy(in_hbm, in_ref, sems.at[3])
    enter.start()
    loads = [pltpu.make_async_copy(table_hbm.at[i], table_ref.at[i], sems.at[i]) for i in range(2)]
    leave = pltpu.make_async_copy(grid_ref, grid_hbm, sems.at[2])
    for load in loads:
        load.start()
    count = own_count(row_lat_ref, lon_count_ref)
    quarter = count // 4
    length = count.astype(f32)
    whole = jnp.full((1, LANES), length)
    shrink = lax.rsqrt(whole)
    groups = order_ref.shape[0]
    pairs = groups * LANES
    order = jnp.concatenate([upright_column(order_ref[pl.ds(i, 1), :]) for i in range(groups)], axis=0)
    swap = remainder(order, 2.0) < 0.5
    even = jnp.where(swap, order, TRUNC - order)
    odd = TRUNC - even
    left = lax.broadcasted_iota(jnp.int32, (pairs, LANES), 1) < 64
    sign_even = jnp.where(remainder(even, 4.0) < 0.5, 1.0, -1.0)
    keep_even = jnp.where(2.0 * even < length, jnp.where(even < 0.5, 1.0, 2.0), 0.0)
    keep_odd = jnp.where(2.0 * odd < length, 2.0, 0.0)
    enter.wait()
    rows_ref[...] = in_ref[...].astype(f32)

    def arrived(s):
        parts = [rows_ref[pl.ds(2 * i + s, LANES, stride=2 * groups), :] for i in range(groups)]
        return jnp.concatenate(parts, axis=0)

    first = arrived(0)
    second = arrived(1)
    coef_even = jnp.where(swap, first, second) * keep_even
    coef_odd = jnp.where(swap, second, first) * keep_odd
    turned_even = pltpu.roll(coef_even, 64, 1)
    turned_odd = pltpu.roll(coef_odd, 64, 1)
    even_cos = jnp.where(left, coef_even, turned_even * sign_even)
    even_sin = -jnp.where(left, turned_even, coef_even * sign_even)
    odd_cos = jnp.where(left, coef_odd, -coef_odd)
    odd_sin = turned_odd

    eye = lax.broadcasted_iota(jnp.int32, (LANES, LANES), 0) == lax.broadcasted_iota(jnp.int32, (LANES, LANES), 1)
    eye = jnp.where(eye, 1.0, 0.0).astype(bf16)

    def upright(values):
        return lax.dot_general(eye, values.astype(bf16), NT, preferred_element_type=f32).astype(bf16)

    waves = (
        (even_cos, odd_cos, odd_cos * sign_even),
        (even_sin, odd_sin, odd_sin * sign_even),
    )
    sums = 0.0
    for i in range(2):
        values = jnp.concatenate([upright(wave) for wave in waves[i]], axis=0)
        loads[i].wait()
        sums += jnp.dot(values, table_ref[i], preferred_element_type=f32)

    width = QUARTER * LANES
    along = lax.broadcasted_iota(jnp.int32, (1, width), 1)
    factor = jnp.where(along < quarter, jnp.broadcast_to(shrink[:, :1], (1, width)), 0.0)
    place_along = along.astype(f32)
    cos_phase, sin_phase = turn(length, remainder(place_along * float(TRUNC), length))
    sum_even = sums[:128]
    sum_odd = jnp.concatenate(
        [
            cos_phase * sums[128:192] + sin_phase * sums[192:256],
            sin_phase * sums[256:320] - cos_phase * sums[320:],
        ],
        axis=0,
    )
    near = (sum_even + sum_odd) * factor
    far = (sum_even - sum_odd) * factor

    place[...] = jnp.zeros_like(place)
    narrow = lax.broadcasted_iota(jnp.int32, (64, LANES), 1)
    for t, field in enumerate((near[:64], near[64:], far[:64], far[64:])):
        start = t * quarter
        shift = start % LANES
        base = start // LANES
        before = jnp.zeros((64, LANES), f32)
        for b in range(QUARTER + 1):
            if b < QUARTER:
                block = field[:, b * LANES : (b + 1) * LANES]
                block = pltpu.roll(block, shift, 1)
            else:
                block = jnp.zeros((64, LANES), f32)
            merged = jnp.where(narrow < shift, before, block)
            at = pl.ds(pl.multiple_of((base + b) * LANES, LANES), LANES)
            place[:, at] += merged
            before = block
    grid_ref[:, 0, :] = place[:, :WIDTH]
    leave.start()

    def product(field):
        return jnp.concatenate(
            [
                half * jnp.concatenate([half[1:], half[:1]], axis=0)
                for half in (field[:64], field[64:])
            ],
            axis=0,
        )

    near = product(near)
    far = product(far)
    both = near + far
    gap = near - far
    first_cos, first_sin = cos_phase * gap[:64], sin_phase * gap[:64]
    second_cos, second_sin = cos_phase * gap[64:], sin_phase * gap[64:]

    def analyse(index, *parts):
        parts = jnp.concatenate(parts, axis=0).astype(bf16)
        return lax.dot_general(table_ref[index], parts, NT, preferred_element_type=f32)

    by_cos = analyse(0, both, first_cos, -first_sin, second_sin, second_cos)
    by_sin = analyse(1, both, first_sin, first_cos, -second_cos, second_sin)
    x_cos, x_sin = by_cos[:, :LANES], by_sin[:, :LANES]
    y_plain = by_cos[:, LANES : 2 * LANES] + by_sin[:, LANES : 2 * LANES]
    y_signed = by_cos[:, 2 * LANES :] + by_sin[:, 2 * LANES :]
    scale = weight_ref[own_place()[0]] * shrink
    back_even = jnp.where(
        left,
        x_cos + sign_even * pltpu.roll(x_cos, 64, 1),
        -(sign_even * x_sin + pltpu.roll(x_sin, 64, 1)),
    )
    back_odd = y_plain + sign_even * y_signed
    back_even = jnp.where(keep_even > 0.0, back_even * scale, 0.0)
    back_odd = jnp.where(keep_odd > 0.0, back_odd * scale, 0.0)
    leaving = (jnp.where(swap, back_even, back_odd), jnp.where(swap, back_odd, back_even))
    for s in range(2):
        for i in range(groups):
            part = leaving[s][i * LANES : (i + 1) * LANES]
            rows_ref[pl.ds(2 * i + s, LANES, stride=2 * groups), :] = part
    back_ref[...] = rows_ref[...].astype(bf16)
    leave.wait()


def grid_step(row_lat, lon_count, weights, order, table, coeffs):
    rows = 2 * order.size
    smem = pl.BlockSpec(memory_space=pltpu.SMEM)
    vmem = pl.BlockSpec(memory_space=pltpu.VMEM)
    return pl.pallas_call(
        grid_kernel,
        in_specs=[smem, smem, smem, vmem, pl.BlockSpec(memory_space=pltpu.HBM), pl.BlockSpec(memory_space=pl.ANY)],
        out_specs=[pl.BlockSpec(memory_space=pltpu.HBM), vmem],
        out_shape=[
            jax.ShapeDtypeStruct((64, 1, WIDTH), f32),
            jax.ShapeDtypeStruct((rows, LANES), bf16),
        ],
        scratch_shapes=[
            pltpu.VMEM((64, (4 * QUARTER + 2) * LANES), f32),
            pltpu.VMEM((rows, LANES), f32),
            pltpu.VMEM(table.shape, bf16),
            pltpu.VMEM((64, 1, WIDTH), f32),
            pltpu.VMEM(coeffs.shape, bf16),
            pltpu.SemaphoreType.DMA((4,)),
        ],
        compiler_params=params(60),
        name="grid",
    )(row_lat, lon_count, weights, order, table, coeffs)


def shards(spectral_in, legendre, weights, pair_order, row_lat, lon_count):
    band_count = lax.axis_size("band")
    lev_count = lax.axis_size("lev")
    devices = band_count * lev_count
    pairs = legendre.shape[0] // lev_count
    all_pairs = pair_order.shape[0]

    def exchange_pairs(blocks):
        rows = blocks.reshape(lev_count, -1, LANES)
        backwards = [list(reversed(range(lev_count)))]
        rows = lax.all_to_all(rows, "lev", 0, 0, tiled=True, axis_index_groups=backwards)
        return rows.reshape(blocks.shape)

    def exchange_rows(rows):
        rows = rows.reshape(devices, pairs, 2, LANES).transpose(0, 2, 1, 3).reshape(devices, 2, -1)
        rows = lax.all_to_all(rows, ("lev", "band"), 0, 0, tiled=True).reshape(devices, 2, pairs, LANES)
        return rows.transpose(0, 2, 1, 3).reshape(2 * all_pairs, LANES)

    buffer = exchange_pairs(pack(legendre, spectral_in))
    fourier = invert(pair_order, buffer)
    fourier, arrived, row_lat, lon_count = lax.optimization_barrier((fourier, pair_order, row_lat, lon_count))
    arrived = arrived.reshape(band_count, lev_count, pairs).transpose(2, 1, 0).reshape(pairs, devices)
    table = basis(row_lat, lon_count, arrived)
    fourier = exchange_rows(fourier)
    grid_row, back = grid_step(row_lat, lon_count, weights, arrived, table, fourier)
    spectral = exchange_pairs(contract(pair_order, buffer, exchange_rows(back)))
    return (grid_row, unpack(spectral, pairs))


def solution(mesh):
    return jax.shard_map(
        shards,
        mesh=mesh,
        in_specs=(P("lev", "band", None, None), P("band", "lev", None), P("lev"), P(), P(), P()),
        out_specs=(P(None, ("lev", "band"), None), P("lev", "band", None, None)),
        check_vma=False,
    )
```

```python
import functools
import math

import jax
import jax.numpy as jnp
from jax import lax
from jax.experimental import pallas as pl
from jax.experimental.pallas import tpu as pltpu
from jax.sharding import PartitionSpec as P

TRUNC = 1279
COEFS = TRUNC + 2
LANES = 128
BLOCKS = (COEFS - 1) // LANES
QUARTER = 11
WIDTH = 4 * TRUNC + 20

f32 = jnp.float32
bf16 = jnp.bfloat16

NT = (((1,), (1,)), ((), ()))


def params(mib=32):
    return pltpu.CompilerParams(vmem_limit_bytes=int(mib * 1024 * 1024))


def own_place():
    return lax.axis_index("band"), lax.axis_index("lev")


def own_split(order_ref, pairs, p):
    band, lev = own_place()
    return TRUNC + 1 - order_ref[(band * lax.axis_size("lev") + lev) * pairs + p]


def own_count(row_lat_ref, lon_count_ref):
    band, lev = own_place()
    return lon_count_ref[row_lat_ref[lev * lax.axis_size("band") + band]]


def pick_matrix():
    row = lax.broadcasted_iota(jnp.int32, (LANES, LANES), 0)
    lane = lax.broadcasted_iota(jnp.int32, (LANES, LANES), 1)
    return jnp.where(row == 2 * (lane % 64) + lane // 64, 1.0, 0.0).astype(bf16)


def pack_kernel(leg_hbm, spec_hbm, out_hbm, leg_ref, spec_ref, out_ref, in_sems, out_sems):
    dests = out_ref.shape[0]
    pairs = leg_ref.shape[0] // dests
    steps = in_sems.shape[0]
    size = leg_ref.shape[0] // steps
    loads, stores = [], []
    for i in range(steps):
        part = pl.ds(i * size, size)
        loads.append(
            (
                pltpu.make_async_copy(leg_hbm.at[part], leg_ref.at[part], in_sems.at[i, 0]),
                pltpu.make_async_copy(spec_hbm.at[:, part], spec_ref.at[:, part], in_sems.at[i, 1]),
            )
        )
        part = pl.ds(dests - (i + 1) * (dests // steps), dests // steps)
        stores.append(pltpu.make_async_copy(out_ref.at[part], out_hbm.at[part], out_sems.at[i]))
    for pair in loads:
        for copy in pair:
            copy.start()
    lane = lax.broadcasted_iota(jnp.int32, (16, LANES), 1)
    for i in range(steps):
        for copy in loads[i]:
            copy.wait()
        for d in range(i * (dests // steps), (i + 1) * (dests // steps)):
            tail = jnp.zeros((16, LANES), f32)
            for p in range(pairs):
                at = d * pairs + p
                table = leg_ref[at].astype(f32)
                spec = jnp.concatenate([spec_ref[l, at].astype(f32) for l in range(4)], axis=0)
                rows = jnp.concatenate([table, spec], axis=0)
                for b in range(BLOCKS):
                    out_ref[dests - 1 - d, p * BLOCKS + b] = rows[:, b * LANES : (b + 1) * LANES].astype(bf16)
                tail = jnp.where(lane == p, rows[:, COEFS - 1 : COEFS], tail)
            out_ref[dests - 1 - d, pairs * BLOCKS] = tail.astype(bf16)
        stores[i].start()
    for store in stores:
        store.wait()


def pack(legendre, spectral):
    pairs = legendre.shape[0] // 16
    out = jax.ShapeDtypeStruct((16, pairs * BLOCKS + 1, 16, LANES), bf16)
    hbm = pl.BlockSpec(memory_space=pltpu.HBM)
    return pl.pallas_call(
        pack_kernel,
        in_specs=[hbm, hbm],
        out_specs=hbm,
        out_shape=out,
        scratch_shapes=[
            pltpu.VMEM(legendre.shape, bf16),
            pltpu.VMEM(spectral.shape, bf16),
            pltpu.VMEM(out.shape, bf16),
            pltpu.SemaphoreType.DMA((8, 2)),
            pltpu.SemaphoreType.DMA((8,)),
        ],
        compiler_params=params(60),
        name="pack",
    )(legendre, spectral)


def halves(buffer_ref, p, which):
    end = buffer_ref.shape[1] - 1
    parts = [buffer_ref[:, p * BLOCKS + b] for b in range(BLOCKS)] + [buffer_ref[:, end]]
    first = which * 8

    def rows(part):
        part = part.astype(f32)[:, first : first + 8]
        return jnp.concatenate([part[d] for d in reversed(range(part.shape[0]))], axis=0).astype(bf16)

    return jnp.concatenate([rows(part) for part in parts], axis=1)


def invert_kernel(order_ref, buffer_ref, out_ref, rows_ref):
    pairs = buffer_ref.shape[1] // BLOCKS
    whole = BLOCKS * LANES
    for p in range(pairs):
        split = own_split(order_ref, pairs, p)
        table = halves(buffer_ref, p, 0)
        data = halves(buffer_ref, p, 1)
        slot = lax.broadcasted_iota(jnp.int32, (16, data.shape[1]), 1)
        first = (slot < split) & (slot < whole)
        second = ((slot >= split) & (slot < whole)) | (slot == whole + p)
        apart = data.reshape(8, 16, data.shape[1])
        kept = [(apart * jnp.where(part, 1.0, 0.0).astype(bf16)[None]).reshape(data.shape) for part in (first, second)]
        sums = lax.dot_general(table, jnp.concatenate(kept, axis=0), NT, preferred_element_type=f32)
        for s in range(2):
            rows_ref[pl.ds(2 * p + s, 128, stride=2 * pairs), :] = sums[:, s * LANES : (s + 1) * LANES]
    rows = rows_ref[...].astype(bf16)
    out_ref[...] = jnp.dot(rows, pick_matrix(), preferred_element_type=f32).astype(bf16)


def invert(order, buffer):
    pairs = buffer.shape[1] // BLOCKS
    rows = 2 * pairs * 128
    vmem = pl.BlockSpec(memory_space=pltpu.VMEM)
    return pl.pallas_call(
        invert_kernel,
        in_specs=[pl.BlockSpec(memory_space=pltpu.SMEM), vmem],
        out_specs=vmem,
        out_shape=jax.ShapeDtypeStruct((rows, LANES), bf16),
        scratch_shapes=[pltpu.VMEM((rows, LANES), f32)],
        compiler_params=params(),
        name="invert",
    )(order, buffer)


def contract_kernel(order_ref, buffer_ref, back_ref, out_ref, rows_ref):
    pairs = buffer_ref.shape[1] // BLOCKS
    rows_ref[...] = back_ref[...].astype(f32)
    apart = [rows_ref[pl.ds(i, 128, stride=2 * pairs), :] for i in range(2 * pairs)]
    apart = jnp.concatenate(apart, axis=0).astype(bf16)
    turned = lax.dot_general(pick_matrix(), apart, NT, preferred_element_type=f32).astype(bf16)
    lane = lax.broadcasted_iota(jnp.int32, (LANES, LANES), 1)
    end = jnp.zeros((LANES, LANES), f32)
    for p in range(pairs):
        split = own_split(order_ref, pairs, p)
        data = halves(buffer_ref, p, 0)
        at = 2 * p * LANES
        back = jnp.concatenate([turned[:, at : at + LANES], turned[:, at + LANES : at + 2 * LANES]], axis=0)
        sums = jnp.dot(back, data, preferred_element_type=f32)
        slot = lax.broadcasted_iota(jnp.int32, (LANES, data.shape[1]), 1)
        result = jnp.where(slot < split, sums[:LANES], sums[LANES:])
        for b in range(0, BLOCKS, 2):
            for d in range(16):
                at = slice(d * 8, (d + 1) * 8)
                left = result[at, b * LANES : (b + 1) * LANES]
                right = result[at, (b + 1) * LANES : (b + 2) * LANES]
                both = jnp.concatenate([left, right], axis=0).astype(bf16)
                out_ref[15 - d, p * (BLOCKS // 2) + b // 2] = both
        end = jnp.where(lane == p, sums[LANES:, BLOCKS * LANES :], end)
    for d in range(16):
        last = end[d * 8 : (d + 1) * 8]
        out_ref[15 - d, pairs * (BLOCKS // 2)] = jnp.concatenate([last, last], axis=0).astype(bf16)


def contract(order, buffer, back):
    pairs = buffer.shape[1] // BLOCKS
    out_blocks = pairs * BLOCKS // 2 + 1
    vmem = pl.BlockSpec(memory_space=pltpu.VMEM)
    return pl.pallas_call(
        contract_kernel,
        in_specs=[pl.BlockSpec(memory_space=pltpu.SMEM), vmem, vmem],
        out_specs=vmem,
        out_shape=jax.ShapeDtypeStruct((16, out_blocks, 16, LANES), bf16),
        scratch_shapes=[pltpu.VMEM((2 * pairs * 128, LANES), f32)],
        compiler_params=params(),
        name="contract",
    )(order, buffer, back)


def unpack_kernel(in_ref, out_hbm, rows_ref, out_ref, sems):
    senders = in_ref.shape[0]
    pairs = out_ref.shape[1] // senders
    blocks = in_ref.shape[1]
    ends = (6, 11, 14, senders)
    stores = {}
    for i, end in enumerate(ends):
        start = ends[i - 1] if i else 0
        part = pl.ds(start * pairs, (end - start) * pairs)
        stores[end] = pltpu.make_async_copy(out_ref.at[:, part], out_hbm.at[:, part], sems.at[i])
    for d in range(senders):
        rows = rows_ref.at[d % 2]
        rows[...] = in_ref[senders - 1 - d].astype(f32)
        tails = [rows[blocks - 1, pl.ds(0, 8), :][:, p : p + 1] for p in range(pairs)]
        for p in range(pairs):
            for b in range(BLOCKS):
                for l in range(4):
                    pair = rows[p * (BLOCKS // 2) + b // 2, pl.ds(b % 2 * 8 + 2 * l, 2), :]
                    out_ref[l, d * pairs + p, :, b * LANES : (b + 1) * LANES] = pair
            for l in range(4):
                last = tails[p][2 * l : 2 * l + 2]
                out_ref[l, d * pairs + p, :, COEFS - 1 : COEFS] = last
        if d + 1 in stores:
            stores[d + 1].start()
    for store in stores.values():
        store.wait()


def unpack(buffer, pairs):
    blocks = buffer.shape[1]
    out = jax.ShapeDtypeStruct((4, 16 * pairs, 2, COEFS), f32)
    return pl.pallas_call(
        unpack_kernel,
        in_specs=[pl.BlockSpec(memory_space=pltpu.VMEM)],
        out_specs=pl.BlockSpec(memory_space=pltpu.HBM),
        out_shape=out,
        scratch_shapes=[
            pltpu.VMEM((2, blocks, 16, LANES), f32),
            pltpu.VMEM(out.shape, f32),
            pltpu.SemaphoreType.DMA((4,)),
        ],
        compiler_params=params(),
        name="unpack",
    )(buffer)


def turn(whole, part):
    scaled = part * (4.0 / whole)
    nearest = jnp.floor(scaled + 0.5)
    angle = (scaled - nearest) * (math.pi / 2)
    square = angle * angle
    sine = angle + angle * square * (
        -1.6666654611e-1 + square * (8.3321608736e-3 - 1.9515295891e-4 * square)
    )
    cosine = 1.0 - 0.5 * square + square * square * (
        4.166664568298827e-2 + square * (-1.388731625493765e-3 + 2.443315711809948e-5 * square)
    )
    odd = (nearest == 1.0) | (nearest == 3.0)
    cos_base = jnp.where(odd, sine, cosine)
    sin_base = jnp.where(odd, cosine, sine)
    cos_sign = jnp.where((nearest == 1.0) | (nearest == 2.0), -1.0, 1.0)
    sin_sign = jnp.where((nearest == 2.0) | (nearest == 3.0), -1.0, 1.0)
    return cos_base * cos_sign, sin_base * sin_sign


def remainder(value, whole):
    quotient = jnp.floor(value * (1.0 / whole))
    rest = value - quotient * whole
    rest = jnp.where(rest < 0.0, rest + whole, rest)
    return jnp.where(rest >= whole, rest - whole, rest)


def upright_column(row):
    return jnp.broadcast_to(row.astype(f32), (LANES, LANES)).T


def basis_kernel(row_lat_ref, lon_count_ref, order_ref, out_ref):
    whole = own_count(row_lat_ref, lon_count_ref).astype(f32)
    order = upright_column(order_ref[pl.ds(pl.program_id(0), 1), :])
    wave = jnp.where(remainder(order, 2.0) < 0.5, order, TRUNC - order)
    lane = lax.broadcasted_iota(jnp.int32, (LANES, LANES), 1).astype(f32)
    cos_fine, sin_fine = turn(whole, remainder(wave * lane, whole))
    cos_coarse, sin_coarse = turn(whole, remainder(wave * (lane * 128.0), whole))
    for a in range(QUARTER):
        cos_a = cos_coarse[:, a : a + 1]
        sin_a = sin_coarse[:, a : a + 1]
        at = pl.ds(a * LANES, LANES)
        out_ref[0, :, at] = (cos_a * cos_fine - sin_a * sin_fine).astype(bf16)
        out_ref[1, :, at] = (sin_a * cos_fine + cos_a * sin_fine).astype(bf16)


def basis(row_lat, lon_count, order):
    rows = LANES
    pairs = order.size
    return pl.pallas_call(
        basis_kernel,
        grid=(pairs // rows,),
        in_specs=[
            pl.BlockSpec(memory_space=pltpu.SMEM),
            pl.BlockSpec(memory_space=pltpu.SMEM),
            pl.BlockSpec(order.shape, lambda i: (0, 0)),
        ],
        out_specs=pl.BlockSpec((2, rows, QUARTER * LANES), lambda i: (0, i, 0)),
        out_shape=jax.ShapeDtypeStruct((2, pairs, QUARTER * LANES), bf16),
        compiler_params=params(60),
        cost_estimate=pl.CostEstimate(flops=200_000_000, bytes_accessed=30_000_000, transcendentals=0),
        name="basis",
    )(row_lat, lon_count, order)


def grid_kernel(row_lat_ref, lon_count_ref, weight_ref, order_ref, table_hbm, in_hbm, grid_hbm, back_ref, place, rows_ref, table_ref, grid_ref, in_ref, sems):
    enter = pltpu.make_async_copy(in_hbm, in_ref, sems.at[3])
    enter.start()
    loads = [pltpu.make_async_copy(table_hbm.at[i], table_ref.at[i], sems.at[i]) for i in range(2)]
    leave = pltpu.make_async_copy(grid_ref, grid_hbm, sems.at[2])
    for load in loads:
        load.start()
    count = own_count(row_lat_ref, lon_count_ref)
    quarter = count // 4
    length = count.astype(f32)
    whole = jnp.full((1, LANES), length)
    shrink = lax.rsqrt(whole)
    groups = order_ref.shape[0]
    pairs = groups * LANES
    order = jnp.concatenate([upright_column(order_ref[pl.ds(i, 1), :]) for i in range(groups)], axis=0)
    swap = remainder(order, 2.0) < 0.5
    even = jnp.where(swap, order, TRUNC - order)
    odd = TRUNC - even
    left = lax.broadcasted_iota(jnp.int32, (pairs, LANES), 1) < 64
    sign_even = jnp.where(remainder(even, 4.0) < 0.5, 1.0, -1.0)
    keep_even = jnp.where(2.0 * even < length, jnp.where(even < 0.5, 1.0, 2.0), 0.0)
    keep_odd = jnp.where(2.0 * odd < length, 2.0, 0.0)
    enter.wait()
    rows_ref[...] = in_ref[...].astype(f32)

    def arrived(s):
        parts = [rows_ref[pl.ds(2 * i + s, LANES, stride=2 * groups), :] for i in range(groups)]
        return jnp.concatenate(parts, axis=0)

    first = arrived(0)
    second = arrived(1)
    coef_even = jnp.where(swap, first, second) * keep_even
    coef_odd = jnp.where(swap, second, first) * keep_odd
    turned_even = pltpu.roll(coef_even, 64, 1)
    turned_odd = pltpu.roll(coef_odd, 64, 1)
    even_cos = jnp.where(left, coef_even, turned_even * sign_even)
    even_sin = -jnp.where(left, turned_even, coef_even * sign_even)
    odd_cos = jnp.where(left, coef_odd, -coef_odd)
    odd_sin = turned_odd

    eye = lax.broadcasted_iota(jnp.int32, (LANES, LANES), 0) == lax.broadcasted_iota(jnp.int32, (LANES, LANES), 1)
    eye = jnp.where(eye, 1.0, 0.0).astype(bf16)

    def upright(values):
        return lax.dot_general(eye, values.astype(bf16), NT, preferred_element_type=f32).astype(bf16)

    waves = (
        (even_cos, odd_cos, odd_cos * sign_even),
        (even_sin, odd_sin, odd_sin * sign_even),
    )
    sums = 0.0
    for i in range(2):
        values = jnp.concatenate([upright(wave) for wave in waves[i]], axis=0)
        loads[i].wait()
        sums += jnp.dot(values, table_ref[i], preferred_element_type=f32)

    width = QUARTER * LANES
    along = lax.broadcasted_iota(jnp.int32, (1, width), 1)
    factor = jnp.where(along < quarter, jnp.broadcast_to(shrink[:, :1], (1, width)), 0.0)
    place_along = along.astype(f32)
    cos_phase, sin_phase = turn(length, remainder(place_along * float(TRUNC), length))
    sum_even = sums[:128]
    sum_odd = jnp.concatenate(
        [
            cos_phase * sums[128:192] + sin_phase * sums[192:256],
            sin_phase * sums[256:320] - cos_phase * sums[320:],
        ],
        axis=0,
    )
    near = (sum_even + sum_odd) * factor
    far = (sum_even - sum_odd) * factor

    place[...] = jnp.zeros_like(place)
    narrow = lax.broadcasted_iota(jnp.int32, (64, LANES), 1)
    for t, field in enumerate((near[:64], near[64:], far[:64], far[64:])):
        start = t * quarter
        shift = start % LANES
        base = start // LANES
        before = jnp.zeros((64, LANES), f32)
        for b in range(QUARTER + 1):
            if b < QUARTER:
                block = field[:, b * LANES : (b + 1) * LANES]
                block = pltpu.roll(block, shift, 1)
            else:
                block = jnp.zeros((64, LANES), f32)
            merged = jnp.where(narrow < shift, before, block)
            at = pl.ds(pl.multiple_of((base + b) * LANES, LANES), LANES)
            place[:, at] += merged
            before = block
    grid_ref[:, 0, :] = place[:, :WIDTH]
    leave.start()

    def product(field):
        return jnp.concatenate(
            [
                half * jnp.concatenate([half[1:], half[:1]], axis=0)
                for half in (field[:64], field[64:])
            ],
            axis=0,
        )

    near = product(near)
    far = product(far)
    both = near + far
    gap = near - far
    first_cos, first_sin = cos_phase * gap[:64], sin_phase * gap[:64]
    second_cos, second_sin = cos_phase * gap[64:], sin_phase * gap[64:]

    def analyse(index, *parts):
        parts = jnp.concatenate(parts, axis=0).astype(bf16)
        return lax.dot_general(table_ref[index], parts, NT, preferred_element_type=f32)

    by_cos = analyse(0, both, first_cos, -first_sin, second_sin, second_cos)
    by_sin = analyse(1, both, first_sin, first_cos, -second_cos, second_sin)
    x_cos, x_sin = by_cos[:, :LANES], by_sin[:, :LANES]
    y_plain = by_cos[:, LANES : 2 * LANES] + by_sin[:, LANES : 2 * LANES]
    y_signed = by_cos[:, 2 * LANES :] + by_sin[:, 2 * LANES :]
    scale = weight_ref[own_place()[0]] * shrink
    back_even = jnp.where(
        left,
        x_cos + sign_even * pltpu.roll(x_cos, 64, 1),
        -(sign_even * x_sin + pltpu.roll(x_sin, 64, 1)),
    )
    back_odd = y_plain + sign_even * y_signed
    back_even = jnp.where(keep_even > 0.0, back_even * scale, 0.0)
    back_odd = jnp.where(keep_odd > 0.0, back_odd * scale, 0.0)
    leaving = (jnp.where(swap, back_even, back_odd), jnp.where(swap, back_odd, back_even))
    for s in range(2):
        for i in range(groups):
            part = leaving[s][i * LANES : (i + 1) * LANES]
            rows_ref[pl.ds(2 * i + s, LANES, stride=2 * groups), :] = part
    back_ref[...] = rows_ref[...].astype(bf16)
    leave.wait()


def grid_step(row_lat, lon_count, weights, order, table, coeffs):
    rows = 2 * order.size
    smem = pl.BlockSpec(memory_space=pltpu.SMEM)
    vmem = pl.BlockSpec(memory_space=pltpu.VMEM)
    return pl.pallas_call(
        grid_kernel,
        in_specs=[smem, smem, smem, vmem, pl.BlockSpec(memory_space=pltpu.HBM), pl.BlockSpec(memory_space=pl.ANY)],
        out_specs=[pl.BlockSpec(memory_space=pltpu.HBM), vmem],
        out_shape=[
            jax.ShapeDtypeStruct((64, 1, WIDTH), f32),
            jax.ShapeDtypeStruct((rows, LANES), bf16),
        ],
        scratch_shapes=[
            pltpu.VMEM((64, (4 * QUARTER + 2) * LANES), f32),
            pltpu.VMEM((rows, LANES), f32),
            pltpu.VMEM(table.shape, bf16),
            pltpu.VMEM((64, 1, WIDTH), f32),
            pltpu.VMEM(coeffs.shape, bf16),
            pltpu.SemaphoreType.DMA((4,)),
        ],
        compiler_params=params(60),
        name="grid",
    )(row_lat, lon_count, weights, order, table, coeffs)


def shards(spectral_in, legendre, weights, pair_order, row_lat, lon_count):
    band_count = lax.axis_size("band")
    lev_count = lax.axis_size("lev")
    devices = band_count * lev_count
    pairs = legendre.shape[0] // lev_count
    all_pairs = pair_order.shape[0]

    def exchange_pairs(blocks):
        rows = blocks.reshape(lev_count, -1, LANES)
        backwards = [list(reversed(range(lev_count)))]
        rows = lax.all_to_all(rows, "lev", 0, 0, tiled=True, axis_index_groups=backwards)
        return rows.reshape(blocks.shape)

    def exchange_rows(rows):
        rows = rows.reshape(devices, pairs, 2, LANES).transpose(0, 2, 1, 3).reshape(devices, 2, -1)
        rows = lax.all_to_all(rows, ("lev", "band"), 0, 0, tiled=True).reshape(devices, 2, pairs, LANES)
        return rows.transpose(0, 2, 1, 3).reshape(2 * all_pairs, LANES)

    buffer = exchange_pairs(pack(legendre, spectral_in))
    fourier = invert(pair_order, buffer)
    fourier, arrived, row_lat, lon_count = lax.optimization_barrier((fourier, pair_order, row_lat, lon_count))
    arrived = arrived.reshape(band_count, lev_count, pairs).transpose(2, 1, 0).reshape(pairs, devices)
    table = basis(row_lat, lon_count, arrived)
    fourier = exchange_rows(fourier)
    grid_row, back = grid_step(row_lat, lon_count, weights, arrived, table, fourier)
    spectral = exchange_pairs(contract(pair_order, buffer, exchange_rows(back)))
    return (grid_row, unpack(spectral, pairs))


def solution(mesh):
    return jax.shard_map(
        shards,
        mesh=mesh,
        in_specs=(P("lev", "band", None, None), P("band", "lev", None), P("lev"), P(), P(), P()),
        out_specs=(P(None, ("lev", "band"), None), P("lev", "band", None, None)),
        check_vma=False,
    )
```
